256 devices in a mesh: dp: 64 (over z, x, core), seq: 4 (over y).
Axes of the slice: x: 4, y: 4, z: 8, core: 2. Of those that a mesh axis runs over, the one named last changes fastest.
Arguments:
- qkv: bfloat16 [64, 1024, 4608], P('dp', 'seq'), may hold values from -7 to 7
- grad_in: bfloat16 [64, 256, 4, 1536], P('dp', 'seq'), may hold values from -6 to 6
- counts: int32 [64, 256], P('dp', 'seq'), may hold values from 1 to 4
- segment: int32 [64, 1024], P('dp', 'seq'), may hold values from 0 to 3, never falling along the last dimension, each value on 1 to 512 neighbouring positions
- conv_weight: float32 [31, 1536], replicated, may hold values from -1 to 1
Outputs:
- qkv_grad: bfloat16 [64, 256, 4, 4608], P('dp', 'seq')
- conv_weight_grad: float32 [31, 1536], replicated
The draws below stay inside these ranges and needn't reach their ends.
Inputs may be any that keep to these rules, and one draw needn't show every extreme that they name: `segment`: never falls along time within an owner's recording; each utterance has 1 to 512 frame slots, one exactly that many.
All inputs are finite; a program needn't handle non-finite values.
Results may differ from the reference program's by a relative error of at most 0.025.
Values may be sent and summed in bfloat16 or wider, within the bound.
A program may use at most 128 MiB of HBM per device.

```python
import math
import jax
import jax.numpy as jnp
import numpy as np
from jax import lax

D = 1536
H = 16
DH = 96
KW = 31
SLOT = 4
UTTS = 4
TIME = 1024
N_DP = 64
N_SEQ = 4


def draw_qkv(key, part):
    key = jax.random.fold_in(key, 7)
    first_key = jax.random.fold_in(key, 0)
    array_dims = (N_DP, TIME, 3 * D)
    drawn = jnp.clip(jax.random.normal(first_key, array_dims, jnp.float32), -6.0, 6.0)
    return drawn.astype(jnp.bfloat16)


def with_ends(entries, rng, smallest, largest):
    longest = entries.shape.index(max(entries.shape))
    spots = []
    for shift in (0, 1):
        where = [jax.random.randint(jax.random.fold_in(rng, axis), (), 0, length) for axis, length in enumerate(entries.shape)]
        where[longest] = (where[longest] + shift) % entries.shape[longest]
        spots.append(tuple(where))
    return entries.at[spots[0]].set(smallest).at[spots[1]].set(largest)


def steps_of(own_key, shape, shards, smallest, top_value):
    loudness = 1.0
    for dim, blocks in shards:
        heights = jax.random.uniform(jax.random.fold_in(jax.random.fold_in(own_key, 6), dim), (blocks,), jnp.float32, smallest / len(shards), top_value / len(shards))
        loudness = loudness * jnp.repeat(jnp.exp(heights), shape[dim] // blocks).reshape((-1,) + (1,) * (len(shape) - 1 - dim))
    return loudness


def profile(amount, total, limit, lean):
    loads = [(1 << 20) // math.isqrt(standing ** lean) + 1 for standing in range(2, amount + 1)]
    spare, given = total - limit - (amount - 1), [1] * (amount - 1)
    while spare > 0:
        movable = [i for i in range(amount - 1) if given[i] < limit]
        mass, left = sum([loads[i] for i in movable]), spare
        for i in movable:
            more = min(limit - given[i], max(1, left * loads[i] // mass), spare)
            given[i] = given[i] + more
            spare = spare - more
    return np.array([limit] + given)


def ragged(stream_key, count, total, most, lean):
    if count == 2:
        one = jax.random.randint(stream_key, (), max(1, total - most), min(most, total - 1) + 1)
        return jnp.stack([one, total - one])
    tallies = jnp.asarray(profile(count, total, most, lean), jnp.int32)
    pairs = (count - 1) // 2
    giver, taker = tallies[1:1 + 2 * pairs:2], tallies[2:2 + 2 * pairs:2]
    room = jnp.minimum(giver - 1, most - taker)
    passed = jax.random.randint(jax.random.fold_in(stream_key, 1), (pairs,), 0, 1 << 20) % (room + 1)
    tallies = tallies.at[1:1 + 2 * pairs:2].set(giver - passed).at[2:2 + 2 * pairs:2].set(taker + passed)
    return tallies[jax.random.permutation(jax.random.fold_in(stream_key, 2), count)]


def bell_draw(stream_key, shape, scale, bound, cuts=(), dtype=jnp.bfloat16):
    entries = scale * jax.random.normal(stream_key, shape, jnp.float32)
    if cuts:
        entries = entries * steps_of(stream_key, shape, cuts, -0.22, 0.18)
    return jnp.clip(entries, -bound, bound).astype(dtype)


def setup_inputs(seed: int = 0) -> dict:
    seeds = jax.random.split(jax.random.key(seed), 6)
    qkv = draw_qkv(jax.random.fold_in(seeds[5], 71), 0)
    grad_in = bell_draw(seeds[1], (N_DP, N_SEQ * N_DP, SLOT, D), 1.0, 6.0, ((0, 64), (1, 4)))
    counts = with_ends(jax.random.randint(seeds[2], (N_DP, N_SEQ * N_DP), 1, SLOT + 1), jax.random.fold_in(seeds[2], 1), 1, SLOT).astype(jnp.int32)
    segment = jax.vmap(lambda own: jnp.searchsorted(jnp.cumsum(ragged(own, UTTS, TIME, TIME // 2, 0)), jnp.arange(TIME), side="right"))(jax.random.split(seeds[3], N_DP)).reshape((N_DP, TIME)).astype(jnp.int32)
    conv_weight = bell_draw(seeds[4], (KW, D), KW ** -0.5, 1.0, (), jnp.float32)
    return dict(qkv=qkv, grad_in=grad_in, counts=counts, segment=segment, conv_weight=conv_weight)


masked_score = -1e+30

def to_bf16(values):
    return lax.optimization_barrier(values.astype(jnp.bfloat16)).astype(jnp.float32)

def owner_block(qkv_owner, cotangent, labels, segment_ids, conv_weight):
    score_scale = DH ** (-0.5)
    queries = qkv_owner[:, :D].astype(jnp.float32).reshape(TIME, H, DH)
    keys_all = qkv_owner[:, D:2 * D].astype(jnp.float32).reshape(TIME, H, DH)
    values_all = qkv_owner[:, 2 * D:].astype(jnp.float32).reshape(TIME, H, DH)
    positions = jnp.arange(TIME)
    allowed = (labels[None, :] == segment_ids[:, None] + 1) | (positions[:, None] == positions[None, :])
    scores = jnp.einsum('thd,uhd->htu', queries, keys_all) * score_scale
    scores = jnp.where(allowed[None], scores, masked_score)
    highest = lax.optimization_barrier(jnp.max(scores, -1, keepdims=True))
    row_total = lax.optimization_barrier(jnp.sum(jnp.where(allowed[None], jnp.exp(scores - highest), 0.0), -1, keepdims=True))
    log_total = highest + jnp.log(row_total)
    soft_weights = jnp.where(allowed[None], jnp.exp(scores - log_total), 0.0)
    soft_rounded = to_bf16(soft_weights)
    attended = to_bf16(jnp.einsum('htu,uhd->thd', soft_rounded, values_all)).reshape(TIME, D)
    margin = (KW - 1) // 2
    pad_cot = jnp.pad(cotangent, ((margin, margin), (0, 0)))
    pad_att = jnp.pad(attended, ((margin, margin), (0, 0)))
    pad_lab = jnp.pad(labels, (margin, margin))
    own_ok = labels > 0
    attended_grad = jnp.zeros((TIME, D), jnp.float32)
    weight_rows = []
    for tap_index in range(KW):
        start_cot = 2 * margin - tap_index
        near = (pad_lab[start_cot:start_cot + TIME] == labels) & own_ok
        attended_grad = attended_grad + conv_weight[tap_index][None, :] * jnp.where(near[:, None], pad_cot[start_cot:start_cot + TIME], 0.0)
        close = (pad_lab[tap_index:tap_index + TIME] == labels) & own_ok
        weight_rows.append(lax.optimization_barrier(jnp.sum(jnp.where(close[:, None], cotangent * pad_att[tap_index:tap_index + TIME], 0.0), 0)))
    weight_grad = jnp.stack(weight_rows)
    dout = to_bf16(attended_grad).reshape(TIME, H, DH)
    delta = lax.optimization_barrier(jnp.sum(dout * attended.reshape(TIME, H, DH), -1)).T
    value_grad = jnp.einsum('htu,thd->uhd', soft_rounded, dout)
    prob_grad = jnp.einsum('thd,uhd->htu', dout, values_all)
    score_grad = to_bf16(soft_weights * (prob_grad - delta[:, :, None]) * score_scale)
    query_grad = jnp.einsum('htu,uhd->thd', score_grad, keys_all)
    key_grad = jnp.einsum('htu,thd->uhd', score_grad, queries)
    joined = jnp.concatenate([query_grad.reshape(TIME, D), key_grad.reshape(TIME, D), value_grad.reshape(TIME, D)], 1)
    return (joined.astype(jnp.bfloat16), weight_grad)

def reference(qkv, grad_in, counts, segment, conv_weight):
    blocks = grad_in.reshape(N_DP, N_SEQ, N_DP, SLOT, D).transpose(2, 1, 0, 3, 4).reshape(N_DP, TIME, D)
    block_counts = counts.reshape(N_DP, N_SEQ, N_DP).transpose(2, 1, 0)
    filled = (jnp.arange(SLOT)[None, None, None, :] < block_counts[..., None]).reshape(N_DP, TIME)
    cotangent = jnp.where(filled[..., None], blocks.astype(jnp.float32), 0.0)
    labels = jnp.where(filled, segment + 1, 0).astype(jnp.int32)

    def one_owner(inputs):
        return owner_block(inputs[0], inputs[1], inputs[2], inputs[3], conv_weight)
    joined, weight_grads = lax.map(one_owner, (qkv, cotangent, labels, segment))
    conv_weight_grad = lax.optimization_barrier(jnp.sum(weight_grads, 0)) / math.sqrt(N_DP * SLOT)
    qkv_grad = joined.reshape(N_DP, N_SEQ, N_DP, SLOT, 3 * D).transpose(2, 1, 0, 3, 4).reshape(N_DP, N_SEQ * N_DP, SLOT, 3 * D)
    return (qkv_grad, conv_weight_grad)
```

```python
import functools
import math

import jax
import jax.numpy as jnp
from jax import lax
from jax.experimental import pallas as pl
from jax.experimental.pallas import tpu as pltpu
from jax.sharding import PartitionSpec as P

H = 16

EMPTY = 128.0
EMPTY_ABOVE = 64.0
MASKED = -1e30
LANES = 128
TB = 256
UB = 128
GAP = 16
CH = 128


def dot(a, b, contract):
    return lax.dot_general(a, b, (contract, ((), ())), preferred_element_type=jnp.float32)


def block_kernel(
    time_rows,
    width,
    head_size,
    taps,
    bounds_ref,
    qkv_ref,
    cot_ref,
    seg_ref,
    cw_ref,
    out_ref,
    taps_ref,
    segb,
    labb,
    shifted,
    grad_pad,
    att_pad,
    k_t,
    v_t,
    do_t,
    att_t,
    dq_t,
    dk,
    dv,
    scores,
    probs,
):
    f32, bf16 = jnp.float32, jnp.bfloat16
    margin = (taps - 1) // 2
    heads = width // head_size
    tiles = width // LANES
    scale = head_size ** (-0.5)
    seg_count = 4
    inner = time_rows + GAP * (seg_count - 1)
    rows_all = shifted.shape[1]

    def rows(index, size):
        return pl.ds(pl.multiple_of(index * size, size), size)

    def chunks(count, body):
        def step(index, carry):
            body(index)
            return carry

        lax.fori_loop(0, count, step, 0)

    def make_labels(c):
        here = rows(c, CH)
        across = jnp.broadcast_to(seg_ref[:, here], (CH, CH)).T
        segb[here, :] = across
        got = cot_ref[here, :LANES].astype(f32)
        labb[here, :] = jnp.where(got < EMPTY_ABOVE, across + 1.0, 0.0)

    chunks(time_rows // CH, make_labels)

    def clear(c):
        here = rows(c, 8)
        shifted[0, here, :] = jnp.zeros((8, width), f32)
        att_pad[here, :] = jnp.zeros((8, width), f32)

    chunks(rows_all // 8, clear)

    def spread(c):
        here = rows(c, CH)
        lab = labb[here, :]
        for j in range(tiles):
            cols = pl.ds(j * LANES, LANES)
            val = cot_ref[here, cols].astype(f32)
            for s in range(seg_count):
                there = pl.ds(pl.multiple_of(c * CH + GAP * (s + 1), GAP), CH)
                shifted[0, there, cols] += jnp.where(lab == s + 1.0, val, 0.0)

    chunks(time_rows // CH, spread)

    def shift(c):
        r0 = pl.multiple_of(c * 48, 8)
        for j in range(tiles):
            cols = pl.ds(j * LANES, LANES)
            block = shifted[0, pl.ds(r0, 56), cols]
            for b in range(1, 8):
                shifted[b, pl.ds(r0, 48), cols] = block[b : b + 48]

    chunks((rows_all - 8) // 48, shift)

    def tap_view(w, r0, size, cols):
        offset = margin - w
        a, b = offset // 8, offset % 8
        return shifted[b, pl.ds(pl.multiple_of(r0 + GAP + 8 * a, 8), size), cols]

    def conv(c):
        r0 = c * 32
        for j in range(tiles):
            cols = pl.ds(j * LANES, LANES)
            total = jnp.zeros((32, LANES), f32)
            for w in range(taps):
                total = total + cw_ref[w : w + 1, cols] * tap_view(w, r0, 32, cols)
            grad_pad[pl.ds(pl.multiple_of(r0, 16), 32), cols] = total

    chunks(grad_pad.shape[0] // 32, conv)

    def transposes(c):
        here = rows(c, CH)
        lab = labb[here, :]
        for j in range(tiles):
            cols = pl.ds(j * LANES, LANES)
            total = jnp.zeros((CH, LANES), f32)
            for s in range(seg_count):
                there = pl.ds(pl.multiple_of(c * CH + GAP * s, GAP), CH)
                total = total + jnp.where(lab == s + 1.0, grad_pad[there, cols], 0.0)
            do_t[cols, here] = total.T
            k_t[cols, here] = qkv_ref[here, pl.ds(width + j * LANES, LANES)].astype(f32).T.astype(bf16)
            v_t[cols, here] = qkv_ref[here, pl.ds(2 * width + j * LANES, LANES)].astype(f32).T.astype(bf16)
        dk[here, :] = jnp.zeros((CH, width), f32)
        dv[here, :] = jnp.zeros((CH, width), f32)

    chunks(time_rows // CH, transposes)

    row_index = lax.broadcasted_iota(jnp.int32, (UB, TB), 0)
    col_index = lax.broadcasted_iota(jnp.int32, (UB, TB), 1)
    apart = col_index - row_index
    to_exp2 = scale * math.log2(math.e)

    for h in range(heads):
        first, last = h * head_size, (h + 1) * head_size
        lane0 = first // LANES * LANES
        span = -(-last // LANES) * LANES - lane0
        before, after = first - lane0, lane0 + span - last
        head_rows = pl.ds(first, head_size)
        lane = lax.broadcasted_iota(jnp.int32, (TB, span), 1)
        in_head = (lane >= before) & (lane < before + head_size)

        def time_block(tb, carry):
            here = rows(tb, TB)
            low, high = bounds_ref[tb, 0], bounds_ref[tb, 1]
            q = jnp.where(in_head, qkv_ref[here, pl.ds(lane0, span)], jnp.zeros((), bf16))
            want = seg_ref[:, here] + 1.0

            def score_step(ub, highest):
                keys = rows(ub, UB)
                s = dot(qkv_ref[keys, pl.ds(width + lane0, span)], q, ((1,), (1,)))
                lab = labb[keys, :]
                lab = jnp.concatenate([lab] * (TB // LANES), axis=1)
                ok = (lab == want) | (apart == ub * UB - tb * TB)
                s = jnp.where(ok, s, MASKED)
                scores[keys, :] = s
                return jnp.maximum(highest, jnp.max(s.reshape(UB // 8, 8, TB), axis=0))

            highest = lax.fori_loop(low, high, score_step, jnp.full((8, TB), MASKED, f32))
            highest = jnp.max(highest, axis=0, keepdims=True) * to_exp2

            def soft_step(ub, carry):
                total, att = carry
                keys = rows(ub, UB)
                p = jnp.exp2(scores[keys, :] * to_exp2 - highest)
                total = total + jnp.sum(p.reshape(UB // 8, 8, TB), axis=0)
                p = p.astype(bf16)
                probs[keys, :] = p
                return total, att + dot(v_t[head_rows, keys], p, ((1,), (0,)))

            total, att = lax.fori_loop(
                low, high, soft_step, (jnp.zeros((8, TB), f32), jnp.zeros((head_size, TB), f32))
            )
            inverse = 1.0 / jnp.sum(total, axis=0, keepdims=True)
            att = (att * inverse).astype(bf16).astype(f32)
            att_t[head_rows, here] = att
            do = do_t[head_rows, here].astype(bf16).astype(f32)
            delta = jnp.sum(do * att, axis=0, keepdims=True) * inverse
            do = (do * inverse).astype(bf16)
            parts = [do]
            if before:
                parts = [jnp.zeros((before, TB), bf16)] + parts
            if after:
                parts = parts + [jnp.zeros((after, TB), bf16)]
            do_wide = jnp.concatenate(parts, axis=0)

            def grad_step(ub, dq):
                keys = rows(ub, UB)
                p = probs[keys, :]
                dp = dot(qkv_ref[keys, pl.ds(2 * width + lane0, span)], do_wide, ((1,), (0,)))
                ds = (p.astype(f32) * (dp - delta)).astype(bf16)
                dk[keys, pl.ds(lane0, span)] += dot(ds, q, ((1,), (0,)))
                dv[keys, pl.ds(lane0, span)] += dot(p, do_wide, ((1,), (1,)))
                return dq + dot(k_t[head_rows, keys], ds, ((1,), (0,)))

            dq = lax.fori_loop(low, high, grad_step, jnp.zeros((head_size, TB), f32))
            dq_t[head_rows, here] = dq * scale
            return carry

        lax.fori_loop(0, time_rows // TB, time_block, 0)

    def results(c):
        here = rows(c, CH)
        lab = labb[here, :]
        for j in range(tiles):
            cols = pl.ds(j * LANES, LANES)
            out_ref[here, cols] = dq_t[cols, here].T.astype(bf16)
            out_ref[here, pl.ds(width + j * LANES, LANES)] = (dk[here, cols] * scale).astype(bf16)
            out_ref[here, pl.ds(2 * width + j * LANES, LANES)] = dv[here, cols].astype(bf16)
            val = att_t[cols, here].T
            for s in range(seg_count):
                there = pl.ds(pl.multiple_of(c * CH + GAP * s, GAP), CH)
                att_pad[there, cols] += jnp.where(lab == s + 1.0, val, 0.0)

    chunks(time_rows // CH, results)

    for j in range(tiles):
        cols = pl.ds(j * LANES, LANES)

        def tap_step(c, sums):
            r0 = c * 8
            att = att_pad[pl.ds(pl.multiple_of(r0, 8), 8), cols]
            return tuple(sums[w] + att * tap_view(w, r0, 8, cols) for w in range(taps))

        sums = lax.fori_loop(
            0, inner // 8, tap_step, tuple(jnp.zeros((8, LANES), f32) for _ in range(taps))
        )
        for w in range(taps):
            taps_ref[w : w + 1, cols] = jnp.sum(sums[w], axis=0, keepdims=True)
        taps_ref[taps : taps + 1, cols] = jnp.zeros((1, LANES), f32)


def run_block(bounds, qkv, cot, seg, cw, head_size):
    time_rows, width = cot.shape
    taps = cw.shape[0]
    f32, bf16 = jnp.float32, jnp.bfloat16
    inner = -(-(time_rows + GAP * 3) // 96) * 96
    rows_all = 23 * 48 + 8
    while rows_all < inner + 2 * GAP + 8:
        rows_all += 48
    vmem = pl.BlockSpec(memory_space=pltpu.VMEM)
    return pl.pallas_call(
        functools.partial(block_kernel, time_rows, width, head_size, taps),
        out_shape=(
            jax.ShapeDtypeStruct((time_rows, 3 * width), bf16),
            jax.ShapeDtypeStruct((taps + 1, width), f32),
        ),
        in_specs=[pl.BlockSpec(memory_space=pltpu.SMEM)] + [vmem] * 4,
        out_specs=(vmem, vmem),
        scratch_shapes=[
            pltpu.VMEM((time_rows, LANES), f32),
            pltpu.VMEM((time_rows, LANES), f32),
            pltpu.VMEM((8, rows_all, width), f32),
            pltpu.VMEM((inner, width), f32),
            pltpu.VMEM((rows_all, width), f32),
            pltpu.VMEM((width, time_rows), bf16),
            pltpu.VMEM((width, time_rows), bf16),
            pltpu.VMEM((width, time_rows), f32),
            pltpu.VMEM((width, time_rows), f32),
            pltpu.VMEM((width, time_rows), f32),
            pltpu.VMEM((time_rows, width), f32),
            pltpu.VMEM((time_rows, width), f32),
            pltpu.VMEM((time_rows, TB), f32),
            pltpu.VMEM((time_rows, TB), bf16),
        ],
        compiler_params=pltpu.CompilerParams(vmem_limit_bytes=56 * 1024 * 1024),
        cost_estimate=pl.CostEstimate(
            flops=14 * time_rows * time_rows * width, bytes_accessed=6 * time_rows * width * 2, transcendentals=0
        ),
    )(bounds, qkv, cot, seg, cw)


def local(qkv, grad_in, counts, segment, conv_weight):
    data_size = lax.axis_size("dp")
    time_size = lax.axis_size("seq")
    rows_here = qkv.shape[1]
    width = qkv.shape[2] // 3
    part = width // time_size
    head_size = width // H
    slot_rows = grad_in.shape[2]
    taps = conv_weight.shape[0]
    time_rows = rows_here * time_size

    filled = jnp.arange(slot_rows)[None, :] < counts[0][:, None]
    sent = jnp.where(filled[:, :, None], grad_in[0], jnp.asarray(EMPTY, jnp.bfloat16))
    sent = sent.reshape(data_size, slot_rows, time_size, part).transpose(0, 2, 1, 3)
    cot = lax.all_to_all(
        sent.reshape(data_size * time_size, slot_rows, part), ("dp", "seq"), 0, 0, tiled=True
    )
    cot = cot.reshape(data_size, time_size, slot_rows, part).transpose(1, 0, 2, 3)
    cot = cot.reshape(time_rows, part)

    mine = qkv[0].reshape(rows_here, 3, time_size, part).transpose(2, 0, 1, 3)
    mine = lax.all_to_all(mine.reshape(time_size, rows_here, 3 * part), "seq", 0, 0, tiled=True)
    mine = mine.reshape(time_rows, 3 * part)

    seg = lax.all_to_all(
        jnp.broadcast_to(segment[:, None, :], (time_size, 1, rows_here)), "seq", 0, 0, tiled=True
    ).reshape(time_rows)
    starts = seg[0::TB]
    ends = seg[TB - 1 :: TB]
    low = jnp.sum(seg[None, :] < starts[:, None], axis=1, dtype=jnp.int32)
    high = jnp.sum(seg[None, :] <= ends[:, None], axis=1, dtype=jnp.int32)
    bounds = jnp.stack([low // UB, (high + UB - 1) // UB], axis=1)
    weights = lax.dynamic_slice_in_dim(conv_weight, lax.axis_index("seq") * part, part, 1)

    grads, tap_terms = run_block(
        bounds, mine, cot, seg.astype(jnp.float32)[None, :], weights, head_size
    )

    grads = grads.reshape(time_size, data_size, slot_rows, 3 * part).transpose(1, 0, 2, 3)
    grads = lax.all_to_all(
        grads.reshape(data_size * time_size, slot_rows, 3 * part), ("dp", "seq"), 0, 0, tiled=True
    )
    grads = grads.reshape(data_size, time_size, slot_rows, 3, part).transpose(0, 2, 3, 1, 4)
    qkv_grad = grads.reshape(1, data_size, slot_rows, 3 * width)

    share = tap_terms.size // data_size
    terms = lax.all_to_all(tap_terms.reshape(data_size, 1, share), "dp", 0, 0, tiled=True)
    total = jnp.sum(terms, axis=0) / math.sqrt(data_size * slot_rows)
    total = lax.all_to_all(
        jnp.broadcast_to(total[None], (data_size, 1, share)), "dp", 0, 0, tiled=True
    ).reshape(taps + 1, part)
    total = lax.all_to_all(
        jnp.broadcast_to(total[None], (time_size, taps + 1, part)), "seq", 0, 0, tiled=True
    )
    conv_weight_grad = total.transpose(1, 0, 2).reshape(taps + 1, width)[:taps]
    return (qkv_grad, conv_weight_grad)


def solution(mesh):
    in_specs = (
        P("dp", "seq", None),
        P("dp", "seq", None, None),
        P("dp", "seq"),
        P("dp", "seq"),
        P(),
    )
    out_specs = (P("dp", "seq", None, None), P())
    return jax.shard_map(local, mesh=mesh, in_specs=in_specs, out_specs=out_specs, check_vma=False)
```

```python
import functools
import math

import jax
import jax.numpy as jnp
from jax import lax
from jax.experimental import pallas as pl
from jax.experimental.pallas import tpu as pltpu
from jax.sharding import PartitionSpec as P

H = 16

EMPTY = 128.0
EMPTY_ABOVE = 64.0
MASKED = -1e30
LANES = 128
TB = 512
UB = 256
PAIR = 2
GAP = 16
SEGMENTS = 4
MESH = pl.DeviceIdType.MESH
CH = 128


def dot(a, b, contract):
    return lax.dot_general(a, b, (contract, ((), ())), preferred_element_type=jnp.float32)


def rows(index, size):
    return pl.ds(pl.multiple_of(index * size, size), size)


def chunks(count, body):
    def step(index, carry):
        body(index)
        return carry

    lax.fori_loop(0, count, step, 0)


def make_labels(time_rows, seg_ref, cot_ref, seg_row, labb):
    piece = seg_ref.shape[2]
    for s in range(seg_ref.shape[0]):
        seg_row[:, s * piece : (s + 1) * piece] = seg_ref[s].astype(jnp.float32)

    def step(c):
        here = rows(c, CH)
        across = jnp.broadcast_to(seg_row[:, here], (CH, CH)).T
        got = cot_ref[here, :LANES].astype(jnp.float32)
        labb[here, :] = jnp.where(got < EMPTY_ABOVE, across + 1.0, 0.0)

    chunks(time_rows // CH, step)


def make_shifted(time_rows, tiles, cot_ref, labb, shifted):
    rows_all = shifted.shape[1]

    def clear(c):
        shifted[0, rows(c, 8), :] = jnp.zeros((8, shifted.shape[2]), jnp.float32)

    chunks(rows_all // 8, clear)

    def spread(c):
        here = rows(c, CH)
        lab = labb[here, :]
        for j in range(tiles):
            cols = pl.ds(j * LANES, LANES)
            val = cot_ref[here, cols].astype(jnp.float32)
            for s in range(SEGMENTS):
                there = pl.ds(pl.multiple_of(c * CH + GAP * (s + 1), GAP), CH)
                shifted[0, there, cols] += jnp.where(lab == s + 1.0, val, 0.0)

    chunks(time_rows // CH, spread)

    def shift(c):
        r0 = pl.multiple_of(c * 48, 8)
        for j in range(tiles):
            cols = pl.ds(j * LANES, LANES)
            block = shifted[0, pl.ds(r0, 56), cols]
            for b in range(1, 8):
                shifted[b, pl.ds(r0, 48), cols] = block[b : b + 48]

    chunks((rows_all - 8) // 48, shift)


def tap_view(shifted, margin, w, r0, size, cols):
    offset = margin - w
    a, b = offset // 8, offset % 8
    return shifted[b, pl.ds(pl.multiple_of(r0 + GAP + 8 * a, 8), size), cols]


def block_kernel(
    time_rows,
    width,
    head_size,
    taps,
    qkv_ref,
    cot_ref,
    seg_ref,
    cw_ref,
    k_t,
    v_t,
    out_ref,
    att_ref,
    bounds,
    seg_row,
    labb,
    shifted,
    grad_pad,
    do_t,
    att_t,
    dq_t,
    dk,
    dv,
    scores,
    probs,
):
    f32, bf16 = jnp.float32, jnp.bfloat16
    margin = (taps - 1) // 2
    heads = width // head_size
    tiles = width // LANES
    scale = head_size ** (-0.5)

    make_labels(time_rows, seg_ref, cot_ref, seg_row, labb)
    make_shifted(time_rows, tiles, cot_ref, labb, shifted)

    def conv(c):
        r0 = c * 32
        for j in range(tiles):
            cols = pl.ds(j * LANES, LANES)
            total = jnp.zeros((32, LANES), f32)
            for w in range(taps):
                total = total + cw_ref[w : w + 1, cols] * tap_view(shifted, margin, w, r0, 32, cols)
            grad_pad[pl.ds(pl.multiple_of(r0, 16), 32), cols] = total

    chunks(grad_pad.shape[0] // 32, conv)

    def transposes(c):
        here = rows(c, CH)
        lab = labb[here, :]
        for j in range(tiles):
            cols = pl.ds(j * LANES, LANES)
            total = jnp.zeros((CH, LANES), f32)
            for s in range(SEGMENTS):
                there = pl.ds(pl.multiple_of(c * CH + GAP * s, GAP), CH)
                total = total + jnp.where(lab == s + 1.0, grad_pad[there, cols], 0.0)
            do_t[cols, here] = total.T
        dk[here, :] = jnp.zeros((CH, width), f32)
        dv[here, :] = jnp.zeros((CH, width), f32)

    chunks(time_rows // CH, transposes)

    everywhere = seg_row[...]
    for tb in range(time_rows // TB):
        mine = seg_row[:, tb * TB : (tb + 1) * TB]
        below = jnp.sum(jnp.where(everywhere < jnp.min(mine), 1, 0))
        upto = jnp.sum(jnp.where(everywhere <= jnp.max(mine), 1, 0))
        bounds[tb, 0] = below // UB
        bounds[tb, 1] = (upto + UB - 1) // UB

    cols_here = PAIR * TB
    row_index = lax.broadcasted_iota(jnp.int32, (UB, cols_here), 0)
    col_index = lax.broadcasted_iota(jnp.int32, (UB, cols_here), 1) % TB
    apart = col_index - row_index
    to_exp2 = scale * math.log2(math.e)

    for h0 in range(0, heads, PAIR):
        first, last = h0 * head_size, (h0 + PAIR) * head_size
        lane0 = first // LANES * LANES
        span = -(-last // LANES) * LANES - lane0
        lane = lax.broadcasted_iota(jnp.int32, (TB, span), 1) + lane0
        head_rows = [pl.ds((h0 + n) * head_size, head_size) for n in range(PAIR)]

        def beside(values):
            return jnp.concatenate(values, axis=1)

        def time_block(tb, carry):
            here = rows(tb, TB)
            low, high = bounds[tb, 0], bounds[tb, 1]
            q = qkv_ref[here, pl.ds(lane0, span)]
            q = jnp.concatenate(
                [
                    jnp.where(
                        (lane >= (h0 + n) * head_size) & (lane < (h0 + n + 1) * head_size),
                        q,
                        jnp.zeros((), bf16),
                    )
                    for n in range(PAIR)
                ],
                axis=0,
            )
            want = beside([seg_row[:, here] + 1.0] * PAIR)

            def score_step(ub, highest):
                keys = rows(ub, UB)
                s = dot(qkv_ref[keys, pl.ds(width + lane0, span)], q, ((1,), (1,)))
                lab = beside([labb[keys, :]] * (cols_here // LANES))
                ok = (lab == want) | (apart == ub * UB - tb * TB)
                s = jnp.where(ok, s, MASKED)
                scores[keys, :] = s
                return jnp.maximum(highest, jnp.max(s.reshape(UB // 8, 8, cols_here), axis=0))

            highest = lax.fori_loop(low, high, score_step, jnp.full((8, cols_here), MASKED, f32))
            highest = jnp.max(highest, axis=0, keepdims=True) * to_exp2
            for n in range(PAIR):
                att_t[head_rows[n], here] = jnp.zeros((head_size, TB), f32)
                dq_t[head_rows[n], here] = jnp.zeros((head_size, TB), f32)

            def soft_step(ub, total):
                keys = rows(ub, UB)
                p = jnp.exp2(scores[keys, :] * to_exp2 - highest)
                total = total + jnp.sum(p.reshape(UB // 8, 8, cols_here), axis=0)
                p = p.astype(bf16)
                probs[keys, :] = p
                for n in range(PAIR):
                    att_t[head_rows[n], here] += dot(
                        v_t[head_rows[n], keys], p[:, n * TB : (n + 1) * TB], ((1,), (0,))
                    )
                return total

            total = lax.fori_loop(low, high, soft_step, jnp.zeros((8, cols_here), f32))
            inverse = 1.0 / jnp.sum(total, axis=0, keepdims=True)
            deltas, wide = [], []
            for n in range(PAIR):
                inv = inverse[:, n * TB : (n + 1) * TB]
                att = (att_t[head_rows[n], here] * inv).astype(bf16).astype(f32)
                att_t[head_rows[n], here] = att
                do = do_t[head_rows[n], here].astype(bf16).astype(f32)
                deltas.append(jnp.sum(do * att, axis=0, keepdims=True) * inv)
                before = (h0 + n) * head_size - lane0
                after = span - before - head_size
                parts = [(do * inv).astype(bf16)]
                if before:
                    parts = [jnp.zeros((before, TB), bf16)] + parts
                if after:
                    parts = parts + [jnp.zeros((after, TB), bf16)]
                wide.append(jnp.concatenate(parts, axis=0))
            delta, do_wide = beside(deltas), beside(wide)

            def grad_step(ub, carry):
                keys = rows(ub, UB)
                p = probs[keys, :]
                dp = dot(qkv_ref[keys, pl.ds(2 * width + lane0, span)], do_wide, ((1,), (0,)))
                ds = (p.astype(f32) * (dp - delta)).astype(bf16)
                dk[keys, pl.ds(lane0, span)] += dot(ds, q, ((1,), (0,)))
                dv[keys, pl.ds(lane0, span)] += dot(p, do_wide, ((1,), (1,)))
                for n in range(PAIR):
                    dq_t[head_rows[n], here] += dot(
                        k_t[head_rows[n], keys], ds[:, n * TB : (n + 1) * TB], ((1,), (0,))
                    )
                return carry

            lax.fori_loop(low, high, grad_step, 0)
            return carry

        lax.fori_loop(0, time_rows // TB, time_block, 0)

    def results(c):
        here = rows(c, CH)
        lab = labb[here, :]
        for j in range(tiles):
            cols = pl.ds(j * LANES, LANES)
            out_ref[here, cols] = (dq_t[cols, here] * scale).T.astype(bf16)
            out_ref[here, pl.ds(width + j * LANES, LANES)] = (dk[here, cols] * scale).astype(bf16)
            out_ref[here, pl.ds(2 * width + j * LANES, LANES)] = dv[here, cols].astype(bf16)
            att_ref[here, cols] = att_t[cols, here].T.astype(bf16)

    chunks(time_rows // CH, results)
def flip_kernel(width, qkv_ref, k_t, v_t):
    def step(c):
        here = rows(c, CH)
        for j in range(width // LANES):
            cols = pl.ds(j * LANES, LANES)
            for n, target in ((1, k_t), (2, v_t)):
                target[cols, here] = qkv_ref[here, pl.ds(n * width + j * LANES, LANES)].T

    chunks(qkv_ref.shape[0] // CH, step)


def taps_kernel(time_rows, width, taps, seg_ref, cot_ref, att_ref, taps_ref, seg_row, labb, shifted, att_pad):
    f32 = jnp.float32
    tiles = width // LANES
    margin = (taps - 1) // 2
    inner = time_rows + GAP * (SEGMENTS - 1)
    make_labels(time_rows, seg_ref, cot_ref, seg_row, labb)
    make_shifted(time_rows, tiles, cot_ref, labb, shifted)

    def clear(c):
        att_pad[rows(c, 8), :] = jnp.zeros((8, width), f32)

    chunks(att_pad.shape[0] // 8, clear)

    def spread(c):
        here = rows(c, CH)
        lab = labb[here, :]
        for j in range(tiles):
            cols = pl.ds(j * LANES, LANES)
            val = att_ref[here, cols].astype(f32)
            for s in range(SEGMENTS):
                there = pl.ds(pl.multiple_of(c * CH + GAP * s, GAP), CH)
                att_pad[there, cols] += jnp.where(lab == s + 1.0, val, 0.0)

    chunks(time_rows // CH, spread)

    for j in range(tiles):
        cols = pl.ds(j * LANES, LANES)

        def tap_step(c, sums):
            r0 = c * 8
            att = att_pad[rows(c, 8), cols]
            return tuple(
                sums[w] + att * tap_view(shifted, margin, w, r0, 8, cols) for w in range(taps)
            )

        sums = lax.fori_loop(
            0, inner // 8, tap_step, tuple(jnp.zeros((8, LANES), f32) for _ in range(taps))
        )
        for w in range(taps):
            taps_ref[w : w + 1, cols] = jnp.sum(sums[w], axis=0, keepdims=True)
        taps_ref[taps : taps + 1, cols] = jnp.zeros((1, LANES), f32)


def padded_rows(time_rows):
    inner = -(-(time_rows + GAP * (SEGMENTS - 1)) // 96) * 96
    return inner, inner + 48 + 8


VMEM = pl.BlockSpec(memory_space=pltpu.VMEM)
ANY = pl.BlockSpec(memory_space=pl.ANY)
PARAMS = dict(vmem_limit_bytes=56 * 1024 * 1024)


def cost(flops, size):
    return pl.CostEstimate(flops=flops, bytes_accessed=size, transcendentals=0)


def flip(qkv, width):
    time_rows = qkv.shape[0]
    shape = jax.ShapeDtypeStruct((width, time_rows), jnp.bfloat16)
    return pl.pallas_call(
        functools.partial(flip_kernel, width),
        out_shape=(shape, shape),
        in_specs=[VMEM],
        out_specs=(VMEM, VMEM),
        compiler_params=pltpu.CompilerParams(**PARAMS),
        cost_estimate=cost(0, 16 * time_rows * width),
    )(qkv)


def run_taps(seg, cot, att, taps):
    time_rows, width = cot.shape
    f32 = jnp.float32
    inner, rows_all = padded_rows(time_rows)
    return pl.pallas_call(
        functools.partial(taps_kernel, time_rows, width, taps),
        out_shape=jax.ShapeDtypeStruct((taps + 1, width), f32),
        in_specs=[VMEM] * 3,
        out_specs=VMEM,
        scratch_shapes=[
            pltpu.VMEM((1, time_rows), f32),
            pltpu.VMEM((time_rows, LANES), f32),
            pltpu.VMEM((8, rows_all, width), f32),
            pltpu.VMEM((rows_all, width), f32),
        ],
        compiler_params=pltpu.CompilerParams(**PARAMS),
        cost_estimate=cost(1 << 33, 40 << 20),
    )(seg, cot, att)


def run_block(qkv, cot, seg, cw, k_t, v_t, head_size):
    time_rows, width = cot.shape
    taps = cw.shape[0]
    f32, bf16 = jnp.float32, jnp.bfloat16
    inner, rows_all = padded_rows(time_rows)
    return pl.pallas_call(
        functools.partial(block_kernel, time_rows, width, head_size, taps),
        out_shape=(
            jax.ShapeDtypeStruct((time_rows, 3 * width), bf16),
            jax.ShapeDtypeStruct((time_rows, width), bf16),
        ),
        in_specs=[VMEM] * 6,
        out_specs=(VMEM, VMEM),
        scratch_shapes=[
            pltpu.SMEM((time_rows // TB, 2), jnp.int32),
            pltpu.VMEM((1, time_rows), f32),
            pltpu.VMEM((time_rows, LANES), f32),
            pltpu.VMEM((8, rows_all, width), f32),
            pltpu.VMEM((inner, width), f32),
            pltpu.VMEM((width, time_rows), f32),
            pltpu.VMEM((width, time_rows), f32),
            pltpu.VMEM((width, time_rows), f32),
            pltpu.VMEM((time_rows, width), f32),
            pltpu.VMEM((time_rows, width), f32),
            pltpu.VMEM((time_rows, PAIR * TB), f32),
            pltpu.VMEM((time_rows, PAIR * TB), bf16),
        ],
        compiler_params=pltpu.CompilerParams(**PARAMS),
        cost_estimate=cost(14 * time_rows * time_rows * width, 12 * time_rows * width),
    )(qkv, cot, seg, cw, k_t, v_t)


def barrier(partners):
    sem = pltpu.get_barrier_semaphore()
    for partner in partners:
        pl.semaphore_signal(sem, inc=1, device_id=partner, device_id_type=MESH)
    pl.semaphore_wait(sem, len(partners))


def exchange_kernel(size, part, qkv_ref, seg_ref, out_ref, seg_out, send_sem, recv_sem, own_sem):
    me = lax.axis_index("seq")
    rows_here = qkv_ref.shape[0]
    width = part * size
    to = [lax.rem(me + k, size) for k in range(1, size)]
    barrier([{"seq": d} for d in to])

    def pieces(d):
        def cols(p):
            return pl.ds(pl.multiple_of(p * width + d * part, part), part)

        moves = [(seg_ref.at[0], seg_out.at[me])]
        for p in range(3):
            target = out_ref.at[rows(me, rows_here), pl.ds(p * part, part)]
            moves.append((qkv_ref.at[:, cols(p)], target))
        return moves

    copies = []
    for k in (2, 1, 3) if size == 4 else range(1, size):
        for n, (src, dst) in enumerate(pieces(to[k - 1])):
            copies.append(
                pltpu.make_async_remote_copy(
                    src_ref=src,
                    dst_ref=dst,
                    send_sem=send_sem.at[k - 1, n],
                    recv_sem=recv_sem.at[k - 1, n],
                    device_id={"seq": to[k - 1]},
                    device_id_type=MESH,
                )
            )
            copies[-1].start()
    own = []
    for n, (src, dst) in enumerate(pieces(me)):
        own.append(pltpu.make_async_copy(src, dst, own_sem.at[n]))
        own[-1].start()
    for copy in own + copies:
        copy.wait()


def exchange(qkv, seg, size):
    rows_here, columns = qkv.shape
    part = columns // 3 // size
    return pl.pallas_call(
        functools.partial(exchange_kernel, size, part),
        out_shape=(
            jax.ShapeDtypeStruct((rows_here * size, 3 * part), qkv.dtype),
            jax.ShapeDtypeStruct((size, 1, rows_here), seg.dtype),
        ),
        in_specs=[ANY, ANY],
        out_specs=(ANY, ANY),
        scratch_shapes=[
            pltpu.SemaphoreType.DMA((size - 1, 4)),
            pltpu.SemaphoreType.DMA((size - 1, 4)),
            pltpu.SemaphoreType.DMA((4,)),
        ],
        compiler_params=pltpu.CompilerParams(collective_id=1, has_side_effects=True),
        cost_estimate=cost(0, 64 << 20),
    )(qkv, seg[None])


def reduce_kernel(size, factor, terms_ref, out_ref, near, far, whole, send_sem, recv_sem):
    group = terms_ref.shape[0]
    data, me = lax.axis_index("dp"), lax.axis_index("seq")
    far_me, near_me = data // group, lax.rem(data, group)
    near_to = [lax.rem(near_me + k, group) for k in range(group)]
    far_to = [lax.rem(far_me + k, group) for k in range(group)]
    seq_to = [lax.rem(me + k, size) for k in range(size)]

    def device(z, n, s):
        return {"dp": z * group + n, "seq": s}

    last = [(k, m) for k in range(group) for m in range(size) if k or m]
    barrier(
        [device(far_me, near_to[k], seq_to[m]) for k, m in last]
        + [device(far_to[k], near_me, me) for k in range(1, group)]
    )
    used = [0]

    def send(src, dst, to):
        n = used[0]
        used[0] += 1
        copy = pltpu.make_async_remote_copy(
            src_ref=src,
            dst_ref=dst,
            send_sem=send_sem.at[n],
            recv_sem=recv_sem.at[n],
            device_id=to,
            device_id_type=MESH,
        )
        copy.start()
        return copy

    copies = [
        send(terms_ref.at[near_to[k]], near.at[k - 1], device(far_me, near_to[k], me))
        for k in range(1, group)
    ]
    for copy in copies:
        copy.wait()
    total = terms_ref[near_me]
    for k in range(1, group):
        total = total + near[k - 1]
    far[far_me] = total
    copies = [
        send(far.at[far_me], far.at[far_me], device(far_to[k], near_me, me)) for k in range(1, group)
    ]
    for copy in copies:
        copy.wait()
    total = far[0]
    for k in range(1, group):
        total = total + far[k]
    whole[me, near_me] = total * factor
    copies = [
        send(whole.at[me, near_me], whole.at[me, near_me], device(far_me, near_to[k], seq_to[m]))
        for k, m in last
    ]
    for copy in copies:
        copy.wait()
    out_ref[...] = whole[...]


def reduce_taps(terms, data_size, size, factor):
    taps, part = terms.shape
    group = math.isqrt(data_size)
    piece = (group, taps // group, part)
    sends = 2 * (group - 1) + group * size - 1
    whole = pl.pallas_call(
        functools.partial(reduce_kernel, size, factor),
        out_shape=jax.ShapeDtypeStruct((size,) + piece, terms.dtype),
        in_specs=[VMEM],
        out_specs=VMEM,
        scratch_shapes=[
            pltpu.VMEM(piece, terms.dtype),
            pltpu.VMEM(piece, terms.dtype),
            pltpu.VMEM((size,) + piece, terms.dtype),
            pltpu.SemaphoreType.DMA((sends,)),
            pltpu.SemaphoreType.DMA((sends,)),
        ],
        compiler_params=pltpu.CompilerParams(collective_id=2, has_side_effects=True),
        cost_estimate=cost(1 << 33, 40 << 20),
    )(terms.reshape(piece))
    return whole.reshape(size, taps, part).transpose(1, 0, 2).reshape(taps, size * part)


def gather_kernel(grads_ref, out_ref):
    size, _, _, columns = grads_ref.shape
    part = columns // 3
    for c in range(size):
        for p in range(3):
            out_ref[:, :, pl.ds((p * size + c) * part, part)] = grads_ref[c, :, :, pl.ds(p * part, part)]


def gather_parts(grads, size):
    blocks, slot_rows, columns = grads.shape
    count, step = blocks // size, 16
    return pl.pallas_call(
        gather_kernel,
        out_shape=jax.ShapeDtypeStruct((count, slot_rows, columns * size), grads.dtype),
        grid=(count // step,),
        in_specs=[pl.BlockSpec((size, step, slot_rows, columns), lambda g: (0, g, 0, 0))],
        out_specs=pl.BlockSpec((step, slot_rows, columns * size), lambda g: (g, 0, 0)),
        compiler_params=pltpu.CompilerParams(**PARAMS),
        cost_estimate=cost(0, 4 * blocks * slot_rows * columns),
    )(grads.reshape(size, count, slot_rows, columns))


def local(qkv, grad_in, counts, segment, conv_weight):
    data_size = lax.axis_size("dp")
    time_size = lax.axis_size("seq")
    rows_here = qkv.shape[1]
    width = qkv.shape[2] // 3
    part = width // time_size
    head_size = width // H
    slot_rows = grad_in.shape[2]
    taps = conv_weight.shape[0]
    time_rows = rows_here * time_size

    filled = jnp.arange(slot_rows)[None, :] < counts[0][:, None]
    sent = jnp.where(filled[:, :, None], grad_in[0], jnp.asarray(EMPTY, jnp.bfloat16))
    sent = sent.reshape(data_size, slot_rows, time_size, part).transpose(2, 0, 1, 3)
    cot = lax.all_to_all(
        sent.reshape(time_size * data_size, slot_rows, part), ("seq", "dp"), 0, 0, tiled=True
    )
    cot = cot.reshape(time_rows, part)

    mine, seg = exchange(qkv[0], segment, time_size)
    k_t, v_t = flip(mine, part)
    weights = lax.dynamic_slice_in_dim(conv_weight, lax.axis_index("seq") * part, part, 1)

    grads, att = run_block(mine, cot, seg, weights, k_t, v_t, head_size)
    grads = lax.all_to_all(
        grads.reshape(time_size * data_size, slot_rows, 3 * part), ("seq", "dp"), 0, 0, tiled=True
    )
    qkv_grad = gather_parts(grads, time_size)[None]

    tap_terms = run_taps(seg, cot, att, taps)
    factor = 1.0 / math.sqrt(data_size * slot_rows)
    conv_weight_grad = reduce_taps(tap_terms, data_size, time_size, factor)[:taps]
    return (qkv_grad, conv_weight_grad)


def solution(mesh):
    in_specs = (
        P("dp", "seq", None),
        P("dp", "seq", None, None),
        P("dp", "seq"),
        P("dp", "seq"),
        P(),
    )
    out_specs = (P("dp", "seq", None, None), P())
    return jax.shard_map(local, mesh=mesh, in_specs=in_specs, out_specs=out_specs, check_vma=False)
```

```python
import functools
import math

import jax
import jax.numpy as jnp
from jax import lax
from jax.experimental import pallas as pl
from jax.experimental.pallas import tpu as pltpu
from jax.sharding import PartitionSpec as P

H = 16

EMPTY = 128.0
EMPTY_ABOVE = 64.0
MASKED = -1e30
LANES = 128
TB = 512
UB = 256
PAIR = 2
GAP = 16
SEGMENTS = 4
MESH = pl.DeviceIdType.MESH
CH = 128


def dot(a, b, contract):
    return lax.dot_general(a, b, (contract, ((), ())), preferred_element_type=jnp.float32)


def rows(index, size):
    return pl.ds(pl.multiple_of(index * size, size), size)


def chunks(count, body):
    def step(index, carry):
        body(index)
        return carry

    lax.fori_loop(0, count, step, 0)


def make_labels(time_rows, seg_ref, cot_ref, seg_row, labb):
    piece = seg_ref.shape[2]
    for s in range(seg_ref.shape[0]):
        seg_row[:, s * piece : (s + 1) * piece] = seg_ref[s].astype(jnp.float32)

    def step(c):
        here = rows(c, CH)
        across = jnp.broadcast_to(seg_row[:, here], (CH, CH)).T
        got = cot_ref[here, :LANES].astype(jnp.float32)
        labb[here, :] = jnp.where(got < EMPTY_ABOVE, across + 1.0, 0.0)

    chunks(time_rows // CH, step)


def make_shifted(time_rows, tiles, cot_ref, labb, shifted):
    rows_all = shifted.shape[1]

    def clear(c):
        shifted[0, rows(c, 8), :] = jnp.zeros((8, shifted.shape[2]), jnp.float32)

    chunks(rows_all // 8, clear)

    def spread(c):
        here = rows(c, CH)
        lab = labb[here, :]
        for j in range(tiles):
            cols = pl.ds(j * LANES, LANES)
            val = cot_ref[here, cols].astype(jnp.float32)
            for s in range(SEGMENTS):
                there = pl.ds(pl.multiple_of(c * CH + GAP * (s + 1), GAP), CH)
                shifted[0, there, cols] += jnp.where(lab == s + 1.0, val, 0.0)

    chunks(time_rows // CH, spread)

    def shift(c):
        r0 = pl.multiple_of(c * 48, 8)
        for j in range(tiles):
            cols = pl.ds(j * LANES, LANES)
            block = shifted[0, pl.ds(r0, 56), cols]
            for b in range(1, 8):
                shifted[b, pl.ds(r0, 48), cols] = block[b : b + 48]

    chunks((rows_all - 8) // 48, shift)


def tap_view(shifted, margin, w, r0, size, cols):
    offset = margin - w
    a, b = offset // 8, offset % 8
    return shifted[b, pl.ds(pl.multiple_of(r0 + GAP + 8 * a, 8), size), cols]


def block_kernel(
    time_rows,
    width,
    head_size,
    taps,
    qkv_ref,
    cot_ref,
    seg_ref,
    cw_ref,
    k_t,
    v_t,
    out_ref,
    att_ref,
    bounds,
    seg_row,
    labb,
    shifted,
    grad_pad,
    do_t,
    att_t,
    dq_t,
    dk,
    dv,
    scores,
    probs,
):
    f32, bf16 = jnp.float32, jnp.bfloat16
    margin = (taps - 1) // 2
    heads = width // head_size
    tiles = width // LANES
    scale = head_size ** (-0.5)

    make_labels(time_rows, seg_ref, cot_ref, seg_row, labb)
    make_shifted(time_rows, tiles, cot_ref, labb, shifted)

    def conv(c):
        r0 = c * 32
        for j in range(tiles):
            cols = pl.ds(j * LANES, LANES)
            total = jnp.zeros((32, LANES), f32)
            for w in range(taps):
                total = total + cw_ref[w : w + 1, cols] * tap_view(shifted, margin, w, r0, 32, cols)
            grad_pad[pl.ds(pl.multiple_of(r0, 16), 32), cols] = total

    chunks(grad_pad.shape[0] // 32, conv)

    def transposes(c):
        here = rows(c, CH)
        lab = labb[here, :]
        for j in range(tiles):
            cols = pl.ds(j * LANES, LANES)
            total = jnp.zeros((CH, LANES), f32)
            for s in range(SEGMENTS):
                there = pl.ds(pl.multiple_of(c * CH + GAP * s, GAP), CH)
                total = total + jnp.where(lab == s + 1.0, grad_pad[there, cols], 0.0)
            do_t[cols, here] = total.T
        dk[here, :] = jnp.zeros((CH, width), f32)
        dv[here, :] = jnp.zeros((CH, width), f32)

    chunks(time_rows // CH, transposes)

    everywhere = seg_row[...]
    for tb in range(time_rows // TB):
        mine = seg_row[:, tb * TB : (tb + 1) * TB]
        below = jnp.sum(jnp.where(everywhere < jnp.min(mine), 1, 0))
        upto = jnp.sum(jnp.where(everywhere <= jnp.max(mine), 1, 0))
        bounds[tb, 0] = below // UB
        bounds[tb, 1] = (upto + UB - 1) // UB

    cols_here = PAIR * TB
    row_index = lax.broadcasted_iota(jnp.int32, (UB, cols_here), 0)
    col_index = lax.broadcasted_iota(jnp.int32, (UB, cols_here), 1) % TB
    apart = col_index - row_index
    to_exp2 = scale * math.log2(math.e)

    for h0 in range(0, heads, PAIR):
        first, last = h0 * head_size, (h0 + PAIR) * head_size
        lane0 = first // LANES * LANES
        span = -(-last // LANES) * LANES - lane0
        lane = lax.broadcasted_iota(jnp.int32, (TB, span), 1) + lane0
        head_rows = [pl.ds((h0 + n) * head_size, head_size) for n in range(PAIR)]

        def beside(values):
            return jnp.concatenate(values, axis=1)

        def time_block(tb, carry):
            here = rows(tb, TB)
            low, high = bounds[tb, 0], bounds[tb, 1]
            q = qkv_ref[here, pl.ds(lane0, span)]
            q = jnp.concatenate(
                [
                    jnp.where(
                        (lane >= (h0 + n) * head_size) & (lane < (h0 + n + 1) * head_size),
                        q,
                        jnp.zeros((), bf16),
                    )
                    for n in range(PAIR)
                ],
                axis=0,
            )
            want = beside([seg_row[:, here] + 1.0] * PAIR)

            def score_step(ub, highest):
                keys = rows(ub, UB)
                s = dot(qkv_ref[keys, pl.ds(width + lane0, span)], q, ((1,), (1,)))
                lab = beside([labb[keys, :]] * (cols_here // LANES))
                ok = (lab == want) | (apart == ub * UB - tb * TB)
                s = jnp.where(ok, s, MASKED)
                scores[keys, :] = s
                return jnp.maximum(highest, jnp.max(s.reshape(UB // 8, 8, cols_here), axis=0))

            highest = lax.fori_loop(low, high, score_step, jnp.full((8, cols_here), MASKED, f32))
            highest = jnp.max(highest, axis=0, keepdims=True) * to_exp2
            for n in range(PAIR):
                att_t[head_rows[n], here] = jnp.zeros((head_size, TB), f32)
                dq_t[head_rows[n], here] = jnp.zeros((head_size, TB), f32)

            def soft_step(ub, total):
                keys = rows(ub, UB)
                p = jnp.exp2(scores[keys, :] * to_exp2 - highest)
                total = total + jnp.sum(p.reshape(UB // 8, 8, cols_here), axis=0)
                p = p.astype(bf16)
                probs[keys, :] = p
                for n in range(PAIR):
                    att_t[head_rows[n], here] += dot(
                        v_t[head_rows[n], keys], p[:, n * TB : (n + 1) * TB], ((1,), (0,))
                    )
                return total

            total = lax.fori_loop(low, high, soft_step, jnp.zeros((8, cols_here), f32))
            inverse = 1.0 / jnp.sum(total, axis=0, keepdims=True)
            deltas, wide = [], []
            for n in range(PAIR):
                inv = inverse[:, n * TB : (n + 1) * TB]
                att = (att_t[head_rows[n], here] * inv).astype(bf16).astype(f32)
                att_t[head_rows[n], here] = att
                do = do_t[head_rows[n], here].astype(bf16).astype(f32)
                deltas.append(jnp.sum(do * att, axis=0, keepdims=True) * inv)
                before = (h0 + n) * head_size - lane0
                after = span - before - head_size
                parts = [(do * inv).astype(bf16)]
                if before:
                    parts = [jnp.zeros((before, TB), bf16)] + parts
                if after:
                    parts = parts + [jnp.zeros((after, TB), bf16)]
                wide.append(jnp.concatenate(parts, axis=0))
            delta, do_wide = beside(deltas), beside(wide)

            def grad_step(ub, carry):
                keys = rows(ub, UB)
                p = probs[keys, :]
                dp = dot(qkv_ref[keys, pl.ds(2 * width + lane0, span)], do_wide, ((1,), (0,)))
                ds = (p.astype(f32) * (dp - delta)).astype(bf16)
                dk[keys, pl.ds(lane0, span)] += dot(ds, q, ((1,), (0,)))
                dv[keys, pl.ds(lane0, span)] += dot(p, do_wide, ((1,), (1,)))
                for n in range(PAIR):
                    dq_t[head_rows[n], here] += dot(
                        k_t[head_rows[n], keys], ds[:, n * TB : (n + 1) * TB], ((1,), (0,))
                    )
                return carry

            lax.fori_loop(low, high, grad_step, 0)
            return carry

        lax.fori_loop(0, time_rows // TB, time_block, 0)

    def results(c):
        here = rows(c, CH)
        lab = labb[here, :]
        for j in range(tiles):
            cols = pl.ds(j * LANES, LANES)
            out_ref[here, cols] = (dq_t[cols, here] * scale).T.astype(bf16)
            out_ref[here, pl.ds(width + j * LANES, LANES)] = (dk[here, cols] * scale).astype(bf16)
            out_ref[here, pl.ds(2 * width + j * LANES, LANES)] = dv[here, cols].astype(bf16)
            att_ref[here, cols] = att_t[cols, here].T.astype(bf16)

    chunks(time_rows // CH, results)
def flip_kernel(width, qkv_ref, k_t, v_t):
    def step(c):
        here = rows(c, CH)
        for j in range(width // LANES):
            cols = pl.ds(j * LANES, LANES)
            for n, target in ((1, k_t), (2, v_t)):
                target[cols, here] = qkv_ref[here, pl.ds(n * width + j * LANES, LANES)].T

    chunks(qkv_ref.shape[0] // CH, step)


def taps_kernel(time_rows, width, taps, seg_ref, cot_ref, att_ref, taps_ref, seg_row, labb, shifted, att_pad):
    f32 = jnp.float32
    tiles = width // LANES
    margin = (taps - 1) // 2
    inner = time_rows + GAP * (SEGMENTS - 1)
    make_labels(time_rows, seg_ref, cot_ref, seg_row, labb)
    make_shifted(time_rows, tiles, cot_ref, labb, shifted)

    def clear(c):
        att_pad[rows(c, 8), :] = jnp.zeros((8, width), f32)

    chunks(att_pad.shape[0] // 8, clear)

    def spread(c):
        here = rows(c, CH)
        lab = labb[here, :]
        for j in range(tiles):
            cols = pl.ds(j * LANES, LANES)
            val = att_ref[here, cols].astype(f32)
            for s in range(SEGMENTS):
                there = pl.ds(pl.multiple_of(c * CH + GAP * s, GAP), CH)
                att_pad[there, cols] += jnp.where(lab == s + 1.0, val, 0.0)

    chunks(time_rows // CH, spread)

    for j in range(tiles):
        cols = pl.ds(j * LANES, LANES)

        def tap_step(c, sums):
            r0 = c * 8
            att = att_pad[rows(c, 8), cols]
            return tuple(
                sums[w] + att * tap_view(shifted, margin, w, r0, 8, cols) for w in range(taps)
            )

        sums = lax.fori_loop(
            0, inner // 8, tap_step, tuple(jnp.zeros((8, LANES), f32) for _ in range(taps))
        )
        for w in range(taps):
            taps_ref[w : w + 1, cols] = jnp.sum(sums[w], axis=0, keepdims=True)
        taps_ref[taps : taps + 1, cols] = jnp.zeros((1, LANES), f32)


def padded_rows(time_rows):
    inner = -(-(time_rows + GAP * (SEGMENTS - 1)) // 96) * 96
    return inner, inner + 48 + 8


VMEM = pl.BlockSpec(memory_space=pltpu.VMEM)
ANY = pl.BlockSpec(memory_space=pl.ANY)
PARAMS = dict(vmem_limit_bytes=56 * 1024 * 1024)


def cost(flops, size):
    return pl.CostEstimate(flops=flops, bytes_accessed=size, transcendentals=0)


def flip(qkv, width):
    time_rows = qkv.shape[0]
    shape = jax.ShapeDtypeStruct((width, time_rows), jnp.bfloat16)
    return pl.pallas_call(
        functools.partial(flip_kernel, width),
        out_shape=(shape, shape),
        in_specs=[VMEM],
        out_specs=(VMEM, VMEM),
        compiler_params=pltpu.CompilerParams(**PARAMS),
        cost_estimate=cost(0, 16 * time_rows * width),
    )(qkv)


def run_taps(seg, cot, att, taps):
    time_rows, width = cot.shape
    f32 = jnp.float32
    inner, rows_all = padded_rows(time_rows)
    return pl.pallas_call(
        functools.partial(taps_kernel, time_rows, width, taps),
        out_shape=jax.ShapeDtypeStruct((taps + 1, width), f32),
        in_specs=[VMEM] * 3,
        out_specs=VMEM,
        scratch_shapes=[
            pltpu.VMEM((1, time_rows), f32),
            pltpu.VMEM((time_rows, LANES), f32),
            pltpu.VMEM((8, rows_all, width), f32),
            pltpu.VMEM((rows_all, width), f32),
        ],
        compiler_params=pltpu.CompilerParams(**PARAMS),
        cost_estimate=cost(1 << 33, 40 << 20),
    )(seg, cot, att)


def run_block(qkv, cot, seg, cw, k_t, v_t, head_size):
    time_rows, width = cot.shape
    taps = cw.shape[0]
    f32, bf16 = jnp.float32, jnp.bfloat16
    inner, rows_all = padded_rows(time_rows)
    return pl.pallas_call(
        functools.partial(block_kernel, time_rows, width, head_size, taps),
        out_shape=(
            jax.ShapeDtypeStruct((time_rows, 3 * width), bf16),
            jax.ShapeDtypeStruct((time_rows, width), bf16),
        ),
        in_specs=[VMEM] * 6,
        out_specs=(VMEM, VMEM),
        scratch_shapes=[
            pltpu.SMEM((time_rows // TB, 2), jnp.int32),
            pltpu.VMEM((1, time_rows), f32),
            pltpu.VMEM((time_rows, LANES), f32),
            pltpu.VMEM((8, rows_all, width), f32),
            pltpu.VMEM((inner, width), f32),
            pltpu.VMEM((width, time_rows), f32),
            pltpu.VMEM((width, time_rows), f32),
            pltpu.VMEM((width, time_rows), f32),
            pltpu.VMEM((time_rows, width), f32),
            pltpu.VMEM((time_rows, width), f32),
            pltpu.VMEM((time_rows, PAIR * TB), f32),
            pltpu.VMEM((time_rows, PAIR * TB), bf16),
        ],
        compiler_params=pltpu.CompilerParams(**PARAMS),
        cost_estimate=cost(14 * time_rows * time_rows * width, 12 * time_rows * width),
    )(qkv, cot, seg, cw, k_t, v_t)


def barrier(partners):
    sem = pltpu.get_barrier_semaphore()
    for partner in partners:
        pl.semaphore_signal(sem, inc=1, device_id=partner, device_id_type=MESH)
    pl.semaphore_wait(sem, len(partners))


def everyone(data_size, size, body):
    group = math.isqrt(data_size)
    data, me = lax.axis_index("dp"), lax.axis_index("seq")
    far, near = data // group, lax.rem(data, group)
    spread = [0]
    for k in range(1, group // 2 + 1):
        spread += [k, group - k] if 2 * k < group else [k]

    def step(e, carry):
        n = lax.rem(near + e, group)
        for z in spread:
            for m in range(size):
                to = (lax.rem(far + z, group) * group + n, lax.rem(me + m, size))
                if z or m:
                    body(e, *to)
                else:
                    pl.when(e > 0)(functools.partial(body, e, *to))
        return carry

    lax.fori_loop(0, group, step, 0)


def barrier_all(data_size, size):
    sem = pltpu.get_barrier_semaphore()

    def greet(e, dp, seq):
        pl.semaphore_signal(sem, inc=1, device_id={"dp": dp, "seq": seq}, device_id_type=MESH)

    everyone(data_size, size, greet)
    pl.semaphore_wait(sem, data_size * size - 1)


def arrive_kernel(
    data_size, size, part, qkv_ref, sent_ref, seg_ref, out_ref, cot_ref, seg_out, send_sem, recv_sem, far_sem, own_sem
):
    data, me = lax.axis_index("dp"), lax.axis_index("seq")
    group = math.isqrt(data_size)
    rows_here = qkv_ref.shape[0]
    width = part * size
    slice_rows = rows_here // group
    to = [lax.rem(me + k, size) for k in range(size)]
    barrier_all(data_size, size)

    def cols(p, d):
        return pl.ds(pl.multiple_of(p * width + d * part, part), part)

    def near_copy(k, p, here, there):
        return pltpu.make_async_remote_copy(
            src_ref=qkv_ref.at[here, cols(p, to[k])],
            dst_ref=out_ref.at[there, pl.ds(p * part, part)],
            send_sem=send_sem.at[k - 1, p],
            recv_sem=recv_sem.at[k - 1, p],
            device_id={"seq": to[k]},
            device_id_type=MESH,
        )

    def far_copy(dp, seq):
        return pltpu.make_async_remote_copy(
            src_ref=sent_ref.at[dp, :, pl.ds(pl.multiple_of(seq * part, part), part)],
            dst_ref=cot_ref.at[me * data_size + data],
            send_sem=far_sem.at[0],
            recv_sem=far_sem.at[1],
            device_id={"dp": dp, "seq": seq},
            device_id_type=MESH,
        )

    def seg_copy(k):
        return pltpu.make_async_remote_copy(
            src_ref=seg_ref.at[0],
            dst_ref=seg_out.at[me],
            send_sem=send_sem.at[k - 1, 3],
            recv_sem=recv_sem.at[k - 1, 3],
            device_id={"seq": to[k]},
            device_id_type=MESH,
        )

    for k in range(1, size):
        seg_copy(k).start()
    moves = [(seg_ref.at[0], seg_out.at[me])]
    moves.append((sent_ref.at[data, :, cols(0, me)], cot_ref.at[me * data_size + data]))
    for p in range(3):
        moves.append((qkv_ref.at[:, cols(p, me)], out_ref.at[rows(me, rows_here), pl.ds(p * part, part)]))
    own = [pltpu.make_async_copy(src, dst, own_sem.at[n]) for n, (src, dst) in enumerate(moves)]
    for copy in own:
        copy.start()

    far, near = data // group, lax.rem(data, group)
    spread = [0, 4, 1, 7, 2, 6, 3, 5] if group == 8 else list(range(group))

    def step(e, carry):
        n = lax.rem(near + e, group)
        here = rows(e, slice_rows)
        there = pl.ds(pl.multiple_of(me * rows_here + e * slice_rows, slice_rows), slice_rows)
        near_left = [(k, p) for p in range(3) for k in range(1, size)]
        for z in spread:
            for k, p in near_left[:2]:
                near_copy(k, p, here, there).start()
            near_left = near_left[2:]
            for m in range(size):
                dp, seq = lax.rem(far + z, group) * group + n, to[m]
                if z or m:
                    far_copy(dp, seq).start()
                else:

                    @pl.when(e > 0)
                    def _():
                        far_copy(dp, seq).start()

        return carry

    lax.fori_loop(0, group, step, 0)
    for copy in own:
        copy.wait()
    for k in range(1, size):
        seg_copy(k).wait()
        for p in range(3):
            near_copy(k, p, pl.ds(0, rows_here), rows(me, rows_here)).wait()
    others = cot_ref.at[pl.ds(0, data_size * size - 1)]
    pltpu.make_async_copy(others, others, far_sem.at[0]).wait()
    pltpu.make_async_copy(others, others, far_sem.at[1]).wait()


def arrive(qkv, sent, seg, data_size, size):
    rows_here, columns = qkv.shape
    part = columns // 3 // size
    slot_rows = sent.shape[1]
    return pl.pallas_call(
        functools.partial(arrive_kernel, data_size, size, part),
        out_shape=(
            jax.ShapeDtypeStruct((rows_here * size, 3 * part), qkv.dtype),
            jax.ShapeDtypeStruct((size * data_size, slot_rows, part), sent.dtype),
            jax.ShapeDtypeStruct((size, 1, rows_here), seg.dtype),
        ),
        in_specs=[ANY, ANY, ANY],
        out_specs=(ANY, ANY, ANY),
        scratch_shapes=[
            pltpu.SemaphoreType.DMA((size - 1, 4)),
            pltpu.SemaphoreType.DMA((size - 1, 4)),
            pltpu.SemaphoreType.DMA((2,)),
            pltpu.SemaphoreType.DMA((5,)),
        ],
        compiler_params=pltpu.CompilerParams(collective_id=1, has_side_effects=True),
        cost_estimate=cost(0, 64 << 20),
    )(qkv, sent, seg[None])


def reduce_kernel(size, factor, terms_ref, out_ref, near, far, whole, send_sem, recv_sem):
    group = terms_ref.shape[0]
    data, me = lax.axis_index("dp"), lax.axis_index("seq")
    far_me, near_me = data // group, lax.rem(data, group)
    near_to = [lax.rem(near_me + k, group) for k in range(group)]
    far_to = [lax.rem(far_me + k, group) for k in range(group)]
    seq_to = [lax.rem(me + k, size) for k in range(size)]

    def device(z, n, s):
        return {"dp": z * group + n, "seq": s}

    last = [(k, m) for k in range(group) for m in range(size) if k or m]
    barrier(
        [device(far_me, near_to[k], seq_to[m]) for k, m in last]
        + [device(far_to[k], near_me, me) for k in range(1, group)]
    )
    used = [0]

    def send(src, dst, to):
        n = used[0]
        used[0] += 1
        copy = pltpu.make_async_remote_copy(
            src_ref=src,
            dst_ref=dst,
            send_sem=send_sem.at[n],
            recv_sem=recv_sem.at[n],
            device_id=to,
            device_id_type=MESH,
        )
        copy.start()
        return copy

    copies = [
        send(terms_ref.at[near_to[k]], near.at[k - 1], device(far_me, near_to[k], me))
        for k in range(1, group)
    ]
    for copy in copies:
        copy.wait()
    total = terms_ref[near_me]
    for k in range(1, group):
        total = total + near[k - 1]
    far[far_me] = total
    copies = [
        send(far.at[far_me], far.at[far_me], device(far_to[k], near_me, me)) for k in range(1, group)
    ]
    for copy in copies:
        copy.wait()
    total = far[0]
    for k in range(1, group):
        total = total + far[k]
    whole[me, near_me] = total * factor
    copies = [
        send(whole.at[me, near_me], whole.at[me, near_me], device(far_me, near_to[k], seq_to[m]))
        for k, m in last
    ]
    for copy in copies:
        copy.wait()
    out_ref[...] = whole[...]


def reduce_taps(terms, data_size, size, factor):
    taps, part = terms.shape
    group = math.isqrt(data_size)
    piece = (group, taps // group, part)
    sends = 2 * (group - 1) + group * size - 1
    whole = pl.pallas_call(
        functools.partial(reduce_kernel, size, factor),
        out_shape=jax.ShapeDtypeStruct((size,) + piece, terms.dtype),
        in_specs=[VMEM],
        out_specs=VMEM,
        scratch_shapes=[
            pltpu.VMEM(piece, terms.dtype),
            pltpu.VMEM(piece, terms.dtype),
            pltpu.VMEM((size,) + piece, terms.dtype),
            pltpu.SemaphoreType.DMA((sends,)),
            pltpu.SemaphoreType.DMA((sends,)),
        ],
        compiler_params=pltpu.CompilerParams(collective_id=2, has_side_effects=True),
        cost_estimate=cost(1 << 33, 40 << 20),
    )(terms.reshape(piece))
    return whole.reshape(size, taps, part).transpose(1, 0, 2).reshape(taps, size * part)


def gather_kernel(grads_ref, out_ref):
    size, _, _, columns = grads_ref.shape
    part = columns // 3
    for c in range(size):
        for p in range(3):
            out_ref[:, :, pl.ds((p * size + c) * part, part)] = grads_ref[c, :, :, pl.ds(p * part, part)]


def gather_parts(grads, size):
    blocks, slot_rows, columns = grads.shape
    count, step = blocks // size, 16
    return pl.pallas_call(
        gather_kernel,
        out_shape=jax.ShapeDtypeStruct((count, slot_rows, columns * size), grads.dtype),
        grid=(count // step,),
        in_specs=[pl.BlockSpec((size, step, slot_rows, columns), lambda g: (0, g, 0, 0))],
        out_specs=pl.BlockSpec((step, slot_rows, columns * size), lambda g: (g, 0, 0)),
        compiler_params=pltpu.CompilerParams(**PARAMS),
        cost_estimate=cost(0, 4 * blocks * slot_rows * columns),
    )(grads.reshape(size, count, slot_rows, columns))


def local(qkv, grad_in, counts, segment, conv_weight):
    data_size = lax.axis_size("dp")
    time_size = lax.axis_size("seq")
    rows_here = qkv.shape[1]
    width = qkv.shape[2] // 3
    part = width // time_size
    head_size = width // H
    slot_rows = grad_in.shape[2]
    taps = conv_weight.shape[0]
    time_rows = rows_here * time_size

    filled = jnp.arange(slot_rows)[None, :] < counts[0][:, None]
    sent = jnp.where(filled[:, :, None], grad_in[0], jnp.asarray(EMPTY, jnp.bfloat16))
    mine, cot, seg = arrive(qkv[0], sent, segment, data_size, time_size)
    cot = cot.reshape(time_rows, part)
    k_t, v_t = flip(mine, part)
    weights = lax.dynamic_slice_in_dim(conv_weight, lax.axis_index("seq") * part, part, 1)

    grads, att = run_block(mine, cot, seg, weights, k_t, v_t, head_size)
    grads = lax.all_to_all(
        grads.reshape(time_size * data_size, slot_rows, 3 * part), ("seq", "dp"), 0, 0, tiled=True
    )
    qkv_grad = gather_parts(grads, time_size)[None]

    tap_terms = run_taps(seg, cot, att, taps)
    factor = 1.0 / math.sqrt(data_size * slot_rows)
    conv_weight_grad = reduce_taps(tap_terms, data_size, time_size, factor)[:taps]
    return (qkv_grad, conv_weight_grad)


def solution(mesh):
    in_specs = (
        P("dp", "seq", None),
        P("dp", "seq", None, None),
        P("dp", "seq"),
        P("dp", "seq"),
        P(),
    )
    out_specs = (P("dp", "seq", None, None), P())
    return jax.shard_map(local, mesh=mesh, in_specs=in_specs, out_specs=out_specs, check_vma=False)
```

```python
import functools
import math

import jax
import jax.numpy as jnp
from jax import lax
from jax.experimental import pallas as pl
from jax.experimental.pallas import tpu as pltpu
from jax.sharding import PartitionSpec as P

H = 16

EMPTY = 128.0
EMPTY_ABOVE = 64.0
MASKED = -1e30
LANES = 128
TB = 512
UB = 256
SLICE = 16
PAIR = 2
GAP = 16
SEGMENTS = 4
MESH = pl.DeviceIdType.MESH
CH = 128


def dot(a, b, contract):
    return lax.dot_general(a, b, (contract, ((), ())), preferred_element_type=jnp.float32)


def rows(index, size):
    return pl.ds(pl.multiple_of(index * size, size), size)


def chunks(count, body):
    def step(index, carry):
        body(index)
        return carry

    lax.fori_loop(0, count, step, 0)


def tap_view(shifted, margin, w, r0, size, cols):
    offset = margin - w
    a, b = offset // 8, offset % 8
    return shifted[b, pl.ds(pl.multiple_of(r0 + GAP + 8 * a, 8), size), cols]


def clear(ref):
    def step(c):
        ref[rows(c, 8), :] = jnp.zeros((8, ref.shape[1]), ref.dtype)

    chunks(ref.shape[0] // 8, step)


def spread_rows(value, labb, target, time_rows, shift, tiles):
    def step(c):
        lab = labb[rows(c, CH), :]
        for j in range(tiles):
            val = value(c, j)
            for s in range(SEGMENTS):
                there = pl.ds(pl.multiple_of(c * CH + GAP * (s + shift), GAP), CH)
                target[there, pl.ds(j * LANES, LANES)] += jnp.where(lab == s + 1.0, val, 0.0)

    chunks(time_rows // CH, step)


def convolve(time_rows, tiles, taps, cols_of, cot, seg_ref, cw_ref, seg_row, labb, shifted, grad_pad, do_t):
    f32 = jnp.float32
    margin = (taps - 1) // 2
    slots = cot.shape[1]
    piece = seg_ref.shape[2]
    for s in range(seg_ref.shape[0]):
        seg_row[:, s * piece : (s + 1) * piece] = seg_ref[s].astype(f32)

    def cot_rows(c, j):
        val = cot[rows(c, CH // slots), :, pl.ds(j * LANES, LANES)].astype(f32)
        return val.reshape(CH, LANES)

    def label(c):
        here = rows(c, CH)
        across = jnp.broadcast_to(seg_row[:, here], (CH, CH)).T
        labb[here, :] = jnp.where(cot_rows(c, 0) < EMPTY_ABOVE, across + 1.0, 0.0)

    chunks(time_rows // CH, label)
    spread_rows(cot_rows, labb, shifted.at[0], time_rows, 1, tiles)

    def shift(c):
        r0 = pl.multiple_of(c * 48, 8)
        for j in range(tiles):
            cols = pl.ds(j * LANES, LANES)
            block = shifted[0, pl.ds(r0, 56), cols]
            for b in range(1, 8):
                shifted[b, pl.ds(r0, 48), cols] = block[b : b + 48]

    chunks((shifted.shape[1] - 8) // 48, shift)

    def conv(c):
        r0 = c * 32
        for j in range(tiles):
            cols = pl.ds(j * LANES, LANES)
            total = jnp.zeros((32, LANES), f32)
            for w in range(taps):
                weight = cw_ref[w : w + 1, cols_of(j)]
                total = total + weight * tap_view(shifted, margin, w, r0, 32, cols)
            grad_pad[pl.ds(pl.multiple_of(r0, 16), 32), cols] = total

    chunks(grad_pad.shape[0] // 32, conv)

    def collect(c):
        lab = labb[rows(c, CH), :]
        for j in range(tiles):
            cols = pl.ds(j * LANES, LANES)
            total = jnp.zeros((CH, LANES), f32)
            for s in range(SEGMENTS):
                there = pl.ds(pl.multiple_of(c * CH + GAP * s, GAP), CH)
                total = total + jnp.where(lab == s + 1.0, grad_pad[there, cols], 0.0)
            do_t[cols, rows(c, CH)] = total.T

    chunks(time_rows // CH, collect)


def attend(time_rows, width, head_size, qkv_ref, seg_row, labb, k_t, v_t, do_t, att_t, dq_t, dk, dv, scores, probs):
    f32, bf16 = jnp.float32, jnp.bfloat16
    heads = width // head_size
    scale = head_size ** (-0.5)

    def flip(c):
        here = rows(c, CH)
        for j in range(width // LANES):
            cols = pl.ds(j * LANES, LANES)
            for n, target in ((1, k_t), (2, v_t)):
                target[cols, here] = qkv_ref[here, pl.ds(n * width + j * LANES, LANES)].T

    chunks(time_rows // CH, flip)
    cols_here = PAIR * TB
    row_index = lax.broadcasted_iota(jnp.int32, (UB, cols_here), 0)
    col_index = lax.broadcasted_iota(jnp.int32, (UB, cols_here), 1) % TB
    apart = col_index - row_index
    to_exp2 = scale * math.log2(math.e)

    for h0 in range(0, heads, PAIR):
        first, last = h0 * head_size, (h0 + PAIR) * head_size
        lane0 = first // LANES * LANES
        span = -(-last // LANES) * LANES - lane0
        lane = lax.broadcasted_iota(jnp.int32, (TB, span), 1) + lane0
        head_rows = [pl.ds((h0 + n) * head_size, head_size) for n in range(PAIR)]

        def beside(values):
            return jnp.concatenate(values, axis=1)

        def time_block(tb, carry):
            here = rows(tb, TB)
            low, high = 0, time_rows // UB
            q = qkv_ref[here, pl.ds(lane0, span)]
            q = jnp.concatenate(
                [
                    jnp.where(
                        (lane >= (h0 + n) * head_size) & (lane < (h0 + n + 1) * head_size),
                        q,
                        jnp.zeros((), bf16),
                    )
                    for n in range(PAIR)
                ],
                axis=0,
            )
            want = beside([seg_row[:, here] + 1.0] * PAIR)

            def score_step(ub, highest):
                keys = rows(ub, UB)
                s = dot(qkv_ref[keys, pl.ds(width + lane0, span)], q, ((1,), (1,)))
                lab = beside([labb[keys, :]] * (cols_here // LANES))
                ok = (lab == want) | (apart == ub * UB - tb * TB)
                s = jnp.where(ok, s, MASKED)
                scores[keys, :] = s
                return jnp.maximum(highest, jnp.max(s.reshape(UB // 8, 8, cols_here), axis=0))

            highest = lax.fori_loop(low, high, score_step, jnp.full((8, cols_here), MASKED, f32))
            highest = jnp.max(highest, axis=0, keepdims=True) * to_exp2
            for n in range(PAIR):
                att_t[head_rows[n], here] = jnp.zeros((head_size, TB), f32)
                dq_t[head_rows[n], here] = jnp.zeros((head_size, TB), f32)

            def soft_step(ub, total):
                keys = rows(ub, UB)
                p = jnp.exp2(scores[keys, :] * to_exp2 - highest)
                total = total + jnp.sum(p.reshape(UB // 8, 8, cols_here), axis=0)
                p = p.astype(bf16)
                probs[keys, :] = p
                for n in range(PAIR):
                    att_t[head_rows[n], here] += dot(
                        v_t[head_rows[n], keys], p[:, n * TB : (n + 1) * TB], ((1,), (0,))
                    )
                return total

            total = lax.fori_loop(low, high, soft_step, jnp.zeros((8, cols_here), f32))
            inverse = 1.0 / jnp.sum(total, axis=0, keepdims=True)
            deltas, wide = [], []
            for n in range(PAIR):
                inv = inverse[:, n * TB : (n + 1) * TB]
                att = (att_t[head_rows[n], here] * inv).astype(bf16).astype(f32)
                att_t[head_rows[n], here] = att
                do = do_t[head_rows[n], here].astype(bf16).astype(f32)
                deltas.append(jnp.sum(do * att, axis=0, keepdims=True) * inv)
                before = (h0 + n) * head_size - lane0
                after = span - before - head_size
                parts = [(do * inv).astype(bf16)]
                if before:
                    parts = [jnp.zeros((before, TB), bf16)] + parts
                if after:
                    parts = parts + [jnp.zeros((after, TB), bf16)]
                wide.append(jnp.concatenate(parts, axis=0))
            delta, do_wide = beside(deltas), beside(wide)

            def grad_step(ub, carry):
                keys = rows(ub, UB)
                p = probs[keys, :]
                dp = dot(qkv_ref[keys, pl.ds(2 * width + lane0, span)], do_wide, ((1,), (0,)))
                ds = (p.astype(f32) * (dp - delta)).astype(bf16)
                dk[keys, pl.ds(lane0, span)] += dot(ds, q, ((1,), (0,)))
                dv[keys, pl.ds(lane0, span)] += dot(p, do_wide, ((1,), (1,)))
                for n in range(PAIR):
                    dq_t[head_rows[n], here] += dot(
                        k_t[head_rows[n], keys], ds[:, n * TB : (n + 1) * TB], ((1,), (0,))
                    )
                return carry

            lax.fori_loop(low, high, grad_step, 0)
            return carry

        lax.fori_loop(0, time_rows // TB, time_block, 0)


def block_kernel(
    data_size,
    size,
    head_size,
    factor,
    qkv_ref,
    sent_ref,
    seg_ref,
    cw_ref,
    out_ref,
    taps_ref,
    seg_all,
    mine,
    cot,
    stage,
    seg_row,
    labb,
    shifted,
    grad_pad,
    att_pad,
    k_t,
    v_t,
    do_t,
    att_t,
    dq_t,
    dk,
    dv,
    scores,
    probs,
    terms,
    near_sum,
    far_sum,
    whole,
    own_sem,
    seq_send,
    seq_recv,
    in_send,
    in_recv,
    out_send,
    out_recv,
    tap_send,
    tap_recv,
):
    f32, bf16 = jnp.float32, jnp.bfloat16
    data, me = lax.axis_index("dp"), lax.axis_index("seq")
    group = math.isqrt(data_size)
    far, near = data // group, lax.rem(data, group)
    rows_here = qkv_ref.shape[0]
    time_rows = rows_here * size
    taps = cw_ref.shape[0]
    margin = (taps - 1) // 2
    part = qkv_ref.shape[1] // 3 // size
    width = part * size
    tiles = part // LANES
    slots = cot.shape[1]
    scale = head_size ** (-0.5)
    to = [lax.rem(me + k, size) for k in range(size)]
    far_order = [0]
    for k in range(1, group // 2 + 1):
        far_order += [k, group - k] if 2 * k < group else [k]

    def partners(e, body):
        for z in far_order:
            for m in range(size):
                call = functools.partial(
                    body, lax.rem(far + z, group) * group + lax.rem(near + e, group), m
                )
                if z or m:
                    call()
                else:
                    pl.when(e > 0)(call)

    def loop(first, last, body):
        def step(e, carry):
            body(e)
            return carry

        lax.fori_loop(first, last, step, 0)

    def remote(src, dst, send, recv, dp, seq):
        return pltpu.make_async_remote_copy(
            src_ref=src,
            dst_ref=dst,
            send_sem=send,
            recv_sem=recv,
            device_id={"dp": dp, "seq": seq},
            device_id_type=MESH,
        )

    barrier_sem = pltpu.get_barrier_semaphore()

    def greet(dp, m):
        pl.semaphore_signal(
            barrier_sem, inc=1, device_id={"dp": dp, "seq": to[m]}, device_id_type=MESH
        )

    loop(0, group, lambda e: partners(e, greet))

    def part_cols(p, d):
        return pl.ds(pl.multiple_of(p * width + d * part, part), part)

    slot = me * data_size + data
    moves = [(seg_ref.at[0], seg_all.at[me])]
    moves.append((sent_ref.at[data, :, part_cols(0, me)], cot.at[slot]))
    for p in range(3):
        moves.append(
            (qkv_ref.at[:, part_cols(p, me)], mine.at[rows(me, rows_here), pl.ds(p * part, part)])
        )
    own = [pltpu.make_async_copy(src, dst, own_sem.at[n]) for n, (src, dst) in enumerate(moves)]
    for copy in own:
        copy.start()
    clear(shifted.at[0])
    clear(att_pad)
    clear(dk)
    clear(dv)
    pl.semaphore_wait(barrier_sem, data_size * size - 1)

    def seg_copy(k):
        return remote(
            seg_ref.at[0], seg_all.at[me], seq_send.at[k - 1, 3], seq_recv.at[k - 1, 3], data, to[k]
        )

    def seq_copy(k, p, first, count):
        return remote(
            qkv_ref.at[pl.ds(first, count), part_cols(p, to[k])],
            mine.at[pl.ds(pl.multiple_of(me * rows_here + first, SLICE), count), pl.ds(p * part, part)],
            seq_send.at[k - 1, p],
            seq_recv.at[k - 1, p],
            data,
            to[k],
        )

    def in_copy(dp, m):
        remote(
            sent_ref.at[dp, :, part_cols(0, to[m])], cot.at[slot], in_send.at[m], in_recv.at[m], dp, to[m]
        ).start()

    for k in range(1, size):
        seg_copy(k).start()

    def begin(e):
        for k in range(1, size):
            for p in range(3):
                seq_copy(k, p, pl.multiple_of(e * SLICE, SLICE), SLICE).start()
        partners(e, in_copy)

    loop(0, group, begin)
    early = group * SLICE
    for p in range(3):
        for k in range(1, size):
            seq_copy(k, p, early, rows_here - early).start()

    for copy in own:
        copy.wait()
    for k in range(1, size):
        seg_copy(k).wait()
    for m in range(size):
        got = sent_ref.at[pl.ds(0, data_size if m else data_size - 1), :, pl.ds(0, part)]
        pltpu.make_async_copy(got, got, in_send.at[m]).wait()
        pltpu.make_async_copy(got, got, in_recv.at[m]).wait()

    def cols_of(j):
        return pl.ds(pl.multiple_of(me * part + j * LANES, LANES), LANES)

    convolve(time_rows, tiles, taps, cols_of, cot, seg_all, cw_ref, seg_row, labb, shifted, grad_pad, do_t)
    for k in range(1, size):
        for p in range(3):
            seq_copy(k, p, 0, rows_here).wait()
    attend(
        time_rows, part, head_size, mine, seg_row, labb, k_t, v_t, do_t, att_t, dq_t, dk, dv, scores, probs
    )

    def results(c):
        here, there = rows(c, CH), rows(c, CH // slots)
        for j in range(tiles):
            cols = pl.ds(j * LANES, LANES)
            for p, val in enumerate(
                ((dq_t[cols, here] * scale).T, dk[here, cols] * scale, dv[here, cols])
            ):
                stage[there, :, pl.ds(p * part + j * LANES, LANES)] = val.reshape(
                    CH // slots, slots, LANES
                ).astype(bf16)

    chunks(time_rows // CH, results)

    def out_cols(p):
        return pl.ds(pl.multiple_of((p * size + me) * part, part), part)

    def out_copy(dp, m):
        for p in range(3):
            remote(
                stage.at[to[m] * data_size + dp, :, pl.ds(p * part, part)],
                out_ref.at[data, :, out_cols(p)],
                out_send.at[m, p],
                out_recv.at[m, p],
                dp,
                to[m],
            ).start()

    def leave(e):
        partners(e, out_copy)

    loop(0, group // 2, leave)
    own = [
        pltpu.make_async_copy(
            stage.at[slot, :, pl.ds(p * part, part)], out_ref.at[data, :, out_cols(p)], own_sem.at[p]
        )
        for p in range(3)
    ]
    for copy in own:
        copy.start()

    spread_rows(
        lambda c, j: att_t[pl.ds(j * LANES, LANES), rows(c, CH)].T, labb, att_pad, time_rows, 0, tiles
    )
    inner = time_rows + GAP * (SEGMENTS - 1)
    each = terms.shape[1]
    terms[group - 1] = jnp.zeros(terms.shape[1:], f32)
    for j in range(tiles):
        cols = pl.ds(j * LANES, LANES)

        def tap_step(c, sums):
            att = att_pad[rows(c, 8), cols]
            return tuple(
                sums[w] + att * tap_view(shifted, margin, w, c * 8, 8, cols) for w in range(taps)
            )

        sums = lax.fori_loop(
            0, inner // 8, tap_step, tuple(jnp.zeros((8, LANES), f32) for _ in range(taps))
        )
        for w in range(taps):
            terms[w // each, w % each : w % each + 1, cols] = jnp.sum(sums[w], axis=0, keepdims=True)

    near_to = [lax.rem(near + k, group) for k in range(group)]
    far_to = [lax.rem(far + k, group) for k in range(group)]
    used = [0]

    def tap_copy(src, dst, z, n, m):
        i = used[0]
        used[0] += 1
        copy = remote(src, dst, tap_send.at[i], tap_recv.at[i], z * group + n, to[m])
        copy.start()
        return copy

    copies = [
        tap_copy(terms.at[near_to[k]], near_sum.at[k - 1], far, near_to[k], 0) for k in range(1, group)
    ]
    loop(group // 2, group - 2, leave)
    for copy in copies:
        copy.wait()
    total = terms[near]
    for k in range(1, group):
        total = total + near_sum[k - 1]
    far_sum[far] = total
    copies = [tap_copy(far_sum.at[far], far_sum.at[far], far_to[k], near, 0) for k in range(1, group)]
    loop(group - 2, group, leave)
    for copy in copies:
        copy.wait()
    total = far_sum[0]
    for k in range(1, group):
        total = total + far_sum[k]
    whole[me, near] = total * factor
    copies = [
        tap_copy(whole.at[me, near], whole.at[me, near], far, near_to[k], m)
        for k in range(group)
        for m in range(size)
        if k or m
    ]
    for copy in copies:
        copy.wait()
    taps_ref[...] = whole[...]

    for copy in own:
        copy.wait()
    for m in range(size):
        for p in range(3):
            got = out_ref.at[pl.ds(0, data_size if m else data_size - 1), :, pl.ds(0, part)]
            pltpu.make_async_copy(got, got, out_send.at[m, p]).wait()
            pltpu.make_async_copy(got, got, out_recv.at[m, p]).wait()


VMEM = pl.BlockSpec(memory_space=pltpu.VMEM)
ANY = pl.BlockSpec(memory_space=pl.ANY)


def run_block(qkv, sent, seg, cw, data_size, size, head_size, factor):
    f32, bf16 = jnp.float32, jnp.bfloat16
    rows_here, columns = qkv.shape
    taps = cw.shape[0]
    slots = sent.shape[1]
    time_rows, width = rows_here * size, columns // 3 // size
    inner = -(-(time_rows + GAP * (SEGMENTS - 1)) // 96) * 96
    rows_all = inner + 48 + 8
    group = math.isqrt(data_size)
    piece = (group, (taps + 1) // group, width)
    sends = 2 * (group - 1) + group * size - 1
    dma = pltpu.SemaphoreType.DMA
    return pl.pallas_call(
        functools.partial(block_kernel, data_size, size, head_size, factor),
        out_shape=(
            jax.ShapeDtypeStruct((data_size, slots, columns), bf16),
            jax.ShapeDtypeStruct((size,) + piece, f32),
        ),
        in_specs=[ANY, ANY, ANY, VMEM],
        out_specs=(ANY, VMEM),
        scratch_shapes=[
            pltpu.VMEM((size, 1, rows_here), seg.dtype),
            pltpu.VMEM((time_rows, 3 * width), bf16),
            pltpu.VMEM((data_size * size, slots, width), bf16),
            pltpu.VMEM((data_size * size, slots, 3 * width), bf16),
            pltpu.VMEM((1, time_rows), f32),
            pltpu.VMEM((time_rows, LANES), f32),
            pltpu.VMEM((8, rows_all, width), f32),
            pltpu.VMEM((inner, width), f32),
            pltpu.VMEM((rows_all, width), f32),
            pltpu.VMEM((width, time_rows), bf16),
            pltpu.VMEM((width, time_rows), bf16),
            pltpu.VMEM((width, time_rows), f32),
            pltpu.VMEM((width, time_rows), f32),
            pltpu.VMEM((width, time_rows), f32),
            pltpu.VMEM((time_rows, width), f32),
            pltpu.VMEM((time_rows, width), f32),
            pltpu.VMEM((time_rows, PAIR * TB), f32),
            pltpu.VMEM((time_rows, PAIR * TB), bf16),
            pltpu.VMEM(piece, f32),
            pltpu.VMEM(piece, f32),
            pltpu.VMEM(piece, f32),
            pltpu.VMEM((size,) + piece, f32),
            dma((5,)),
            dma((size - 1, 4)),
            dma((size - 1, 4)),
            dma((size,)),
            dma((size,)),
            dma((size, 3)),
            dma((size, 3)),
            dma((sends,)),
            dma((sends,)),
        ],
        compiler_params=pltpu.CompilerParams(
            collective_id=1, has_side_effects=True, vmem_limit_bytes=58 * 1024 * 1024
        ),
        cost_estimate=pl.CostEstimate(
            flops=14 * time_rows * time_rows * width, bytes_accessed=64 << 20, transcendentals=0
        ),
    )(qkv, sent, seg[None], cw)


def local(qkv, grad_in, counts, segment, conv_weight):
    data_size = lax.axis_size("dp")
    time_size = lax.axis_size("seq")
    width = qkv.shape[2] // 3
    part = width // time_size
    head_size = width // H
    slot_rows = grad_in.shape[2]
    taps = conv_weight.shape[0]

    filled = jnp.arange(slot_rows)[None, :] < counts[0][:, None]
    sent = jnp.where(filled[:, :, None], grad_in[0], jnp.asarray(EMPTY, jnp.bfloat16))
    factor = 1.0 / math.sqrt(data_size * slot_rows)
    grads, total = run_block(
        qkv[0], sent, segment, conv_weight, data_size, time_size, head_size, factor
    )
    total = total.reshape(time_size, taps + 1, part).transpose(1, 0, 2)
    conv_weight_grad = total.reshape(taps + 1, time_size * part)[:taps]
    qkv_grad = grads[None]
    return (qkv_grad, conv_weight_grad)


def solution(mesh):
    in_specs = (
        P("dp", "seq", None),
        P("dp", "seq", None, None),
        P("dp", "seq"),
        P("dp", "seq"),
        P(),
    )
    out_specs = (P("dp", "seq", None, None), P())
    return jax.shard_map(local, mesh=mesh, in_specs=in_specs, out_specs=out_specs, check_vma=False)
```

```python
import functools
import math

import jax
import jax.numpy as jnp
from jax import lax
from jax.experimental import pallas as pl
from jax.experimental.pallas import tpu as pltpu
from jax.sharding import PartitionSpec as P

H = 16

EMPTY = 128.0
EMPTY_ABOVE = 64.0
MASKED = -1e30
LANES = 128
TB = 512
UB = 256
SLICE = 16
PAIR = 2
GAP = 16
SEGMENTS = 4
MESH = pl.DeviceIdType.MESH
CH = 128


def dot(a, b, contract):
    return lax.dot_general(a, b, (contract, ((), ())), preferred_element_type=jnp.float32)


def rows(index, size):
    return pl.ds(pl.multiple_of(index * size, size), size)


def chunks(count, body):
    def step(index, carry):
        body(index)
        return carry

    lax.fori_loop(0, count, step, 0)


def tap_view(shifted, margin, w, r0, size, cols):
    offset = margin - w
    a, b = offset // 8, offset % 8
    return shifted[b, pl.ds(pl.multiple_of(r0 + GAP + 8 * a, 8), size), cols]


def clear(ref):
    def step(c):
        ref[rows(c, 8), :] = jnp.zeros((8, ref.shape[1]), ref.dtype)

    chunks(ref.shape[0] // 8, step)


def spread_rows(value, labb, target, time_rows, shift, tiles):
    def step(c):
        lab = labb[rows(c, CH), :]
        for j in range(tiles):
            val = value(c, j)
            for s in range(SEGMENTS):
                there = pl.ds(pl.multiple_of(c * CH + GAP * (s + shift), GAP), CH)
                target[there, pl.ds(j * LANES, LANES)] += jnp.where(lab == s + 1.0, val, 0.0)

    chunks(time_rows // CH, step)


def convolve(time_rows, tiles, taps, cols_of, cot, seg_ref, cw_ref, seg_row, labb, shifted, grad_pad, do_t):
    f32 = jnp.float32
    margin = (taps - 1) // 2
    slots = cot.shape[1]
    piece = seg_ref.shape[2]
    for s in range(seg_ref.shape[0]):
        seg_row[:, s * piece : (s + 1) * piece] = seg_ref[s].astype(f32)

    def cot_rows(c, j):
        val = cot[rows(c, CH // slots), :, pl.ds(j * LANES, LANES)].astype(f32)
        return val.reshape(CH, LANES)

    def label(c):
        here = rows(c, CH)
        across = jnp.broadcast_to(seg_row[:, here], (CH, CH)).T
        labb[here, :] = jnp.where(cot_rows(c, 0) < EMPTY_ABOVE, across + 1.0, 0.0)

    chunks(time_rows // CH, label)
    spread_rows(cot_rows, labb, shifted.at[0], time_rows, 1, tiles)

    def shift(c):
        r0 = pl.multiple_of(c * 48, 8)
        for j in range(tiles):
            cols = pl.ds(j * LANES, LANES)
            block = shifted[0, pl.ds(r0, 56), cols]
            for b in range(1, 8):
                shifted[b, pl.ds(r0, 48), cols] = block[b : b + 48]

    chunks((shifted.shape[1] - 8) // 48, shift)

    def conv(c):
        r0 = c * 32
        for j in range(tiles):
            cols = pl.ds(j * LANES, LANES)
            total = jnp.zeros((32, LANES), f32)
            for w in range(taps):
                weight = cw_ref[w : w + 1, cols_of(j)]
                total = total + weight * tap_view(shifted, margin, w, r0, 32, cols)
            grad_pad[pl.ds(pl.multiple_of(r0, 16), 32), cols] = total

    chunks(grad_pad.shape[0] // 32, conv)

    def collect(c):
        lab = labb[rows(c, CH), :]
        for j in range(tiles):
            cols = pl.ds(j * LANES, LANES)
            total = jnp.zeros((CH, LANES), f32)
            for s in range(SEGMENTS):
                there = pl.ds(pl.multiple_of(c * CH + GAP * s, GAP), CH)
                total = total + jnp.where(lab == s + 1.0, grad_pad[there, cols], 0.0)
            do_t[cols, rows(c, CH)] = total.T

    chunks(time_rows // CH, collect)


def flip(time_rows, width, tiles, qkv_ref, k_t, v_t):
    def step(c):
        here = rows(c, CH)
        for j in tiles:
            for n, target in ((1, k_t), (2, v_t)):
                block = qkv_ref[here, pl.ds(n * width + j * LANES, LANES)]
                target[pl.ds(j * LANES, LANES), here] = block.T

    chunks(time_rows // CH, step)


def attend(
    h0, time_rows, width, head_size, qkv_ref, seg_row, labb, k_t, v_t, do_t, att_t, dq_t, dk, dv, scores, probs
):
    f32, bf16 = jnp.float32, jnp.bfloat16
    scale = head_size ** (-0.5)
    cols_here = PAIR * TB
    row_index = lax.broadcasted_iota(jnp.int32, (UB, cols_here), 0)
    col_index = lax.broadcasted_iota(jnp.int32, (UB, cols_here), 1) % TB
    apart = col_index - row_index
    to_exp2 = scale * math.log2(math.e)

    first, last = h0 * head_size, (h0 + PAIR) * head_size
    lane0 = first // LANES * LANES
    span = -(-last // LANES) * LANES - lane0
    lane = lax.broadcasted_iota(jnp.int32, (TB, span), 1) + lane0
    head_rows = [pl.ds((h0 + n) * head_size, head_size) for n in range(PAIR)]

    def beside(values):
        return jnp.concatenate(values, axis=1)

    def time_block(tb, carry):
        here = rows(tb, TB)
        q = qkv_ref[here, pl.ds(lane0, span)]
        q = jnp.concatenate(
            [
                jnp.where(
                    (lane >= (h0 + n) * head_size) & (lane < (h0 + n + 1) * head_size),
                    q,
                    jnp.zeros((), bf16),
                )
                for n in range(PAIR)
            ],
            axis=0,
        )
        want = beside([seg_row[:, here] + 1.0] * PAIR)

        def score_step(ub, highest):
            keys = rows(ub, UB)
            s = dot(qkv_ref[keys, pl.ds(width + lane0, span)], q, ((1,), (1,)))
            lab = beside([labb[keys, :]] * (cols_here // LANES))
            ok = (lab == want) | (apart == ub * UB - tb * TB)
            s = jnp.where(ok, s, MASKED)
            scores[keys, :] = s
            return jnp.maximum(highest, jnp.max(s.reshape(UB // 8, 8, cols_here), axis=0))

        highest = lax.fori_loop(0, time_rows // UB, score_step, jnp.full((8, cols_here), MASKED, f32), unroll=True)
        highest = jnp.max(highest, axis=0, keepdims=True) * to_exp2
        for n in range(PAIR):
            att_t[head_rows[n], here] = jnp.zeros((head_size, TB), f32)
            dq_t[head_rows[n], here] = jnp.zeros((head_size, TB), f32)

        def soft_step(ub, total):
            keys = rows(ub, UB)
            p = jnp.exp2(scores[keys, :] * to_exp2 - highest)
            total = total + jnp.sum(p.reshape(UB // 8, 8, cols_here), axis=0)
            p = p.astype(bf16)
            probs[keys, :] = p
            for n in range(PAIR):
                att_t[head_rows[n], here] += dot(
                    v_t[head_rows[n], keys], p[:, n * TB : (n + 1) * TB], ((1,), (0,))
                )
            return total

        total = lax.fori_loop(0, time_rows // UB, soft_step, jnp.zeros((8, cols_here), f32), unroll=True)
        inverse = 1.0 / jnp.sum(total, axis=0, keepdims=True)
        deltas, wide = [], []
        for n in range(PAIR):
            inv = inverse[:, n * TB : (n + 1) * TB]
            att = (att_t[head_rows[n], here] * inv).astype(bf16).astype(f32)
            att_t[head_rows[n], here] = att
            do = do_t[head_rows[n], here].astype(bf16).astype(f32)
            deltas.append(jnp.sum(do * att, axis=0, keepdims=True) * inv)
            before = (h0 + n) * head_size - lane0
            after = span - before - head_size
            parts = [(do * inv).astype(bf16)]
            if before:
                parts = [jnp.zeros((before, TB), bf16)] + parts
            if after:
                parts = parts + [jnp.zeros((after, TB), bf16)]
            wide.append(jnp.concatenate(parts, axis=0))
        delta, do_wide = beside(deltas), beside(wide)

        def grad_step(ub, carry):
            keys = rows(ub, UB)
            p = probs[keys, :]
            dp = dot(qkv_ref[keys, pl.ds(2 * width + lane0, span)], do_wide, ((1,), (0,)))
            ds = (p.astype(f32) * (dp - delta)).astype(bf16)
            dk[keys, pl.ds(lane0, span)] += dot(ds, q, ((1,), (0,)))
            dv[keys, pl.ds(lane0, span)] += dot(p, do_wide, ((1,), (1,)))
            for n in range(PAIR):
                dq_t[head_rows[n], here] += dot(
                    k_t[head_rows[n], keys], ds[:, n * TB : (n + 1) * TB], ((1,), (0,))
                )
            return carry

        lax.fori_loop(0, time_rows // UB, grad_step, 0, unroll=True)
        return carry

    lax.fori_loop(0, time_rows // TB, time_block, 0)


def block_kernel(
    data_size,
    size,
    head_size,
    factor,
    qkv_ref,
    grad_ref,
    counts_ref,
    seg_ref,
    cw_ref,
    out_ref,
    taps_ref,
    seg_all,
    mine,
    sent,
    cot,
    stage,
    seg_row,
    labb,
    shifted,
    grad_pad,
    att_pad,
    k_t,
    v_t,
    do_t,
    att_t,
    dq_t,
    dk,
    dv,
    scores,
    probs,
    terms,
    near_sum,
    far_sum,
    whole,
    own_sem,
    seq_send,
    seq_recv,
    in_send,
    in_recv,
    out_send,
    out_recv,
    tap_send,
    tap_recv,
):
    f32, bf16 = jnp.float32, jnp.bfloat16
    data, me = lax.axis_index("dp"), lax.axis_index("seq")
    group = math.isqrt(data_size)
    far, near = data // group, lax.rem(data, group)
    qkv_ref = qkv_ref.at[0]
    rows_here = qkv_ref.shape[0]
    time_rows = rows_here * size
    taps = cw_ref.shape[0]
    margin = (taps - 1) // 2
    part = qkv_ref.shape[1] // 3 // size
    width = part * size
    tiles = part // LANES
    slots = cot.shape[1]
    scale = head_size ** (-0.5)
    to = [lax.rem(me + k, size) for k in range(size)]
    far_order = [0]
    for k in range(1, group // 2 + 1):
        far_order += [k, group - k] if 2 * k < group else [k]

    def partners(e, body):
        for z in far_order:
            for m in range(size):
                call = functools.partial(
                    body, lax.rem(far + z, group) * group + lax.rem(near + e, group), m
                )
                if z or m:
                    call()
                else:
                    pl.when(e > 0)(call)

    def loop(first, last, body):
        def step(e, carry):
            body(e)
            return carry

        lax.fori_loop(first, last, step, 0)

    def remote(src, dst, send, recv, dp, seq):
        return pltpu.make_async_remote_copy(
            src_ref=src,
            dst_ref=dst,
            send_sem=send,
            recv_sem=recv,
            device_id={"dp": dp, "seq": seq},
            device_id_type=MESH,
        )

    barrier_sem = pltpu.get_barrier_semaphore()

    def greet(dp, m):
        pl.semaphore_signal(
            barrier_sem, inc=1, device_id={"dp": dp, "seq": to[m]}, device_id_type=MESH
        )

    loop(0, group, lambda e: partners(e, greet))

    def part_cols(p, d):
        return pl.ds(pl.multiple_of(p * width + d * part, part), part)

    slot = me * data_size + data
    moves = [(seg_ref.at[0], seg_all.at[me])]
    for p in range(3):
        moves.append(
            (qkv_ref.at[:, part_cols(p, me)], mine.at[rows(me, rows_here), pl.ds(p * part, part)])
        )
    own = [pltpu.make_async_copy(src, dst, own_sem.at[n]) for n, (src, dst) in enumerate(moves)]
    for copy in own:
        copy.start()
    slot_row = lax.broadcasted_iota(jnp.int32, sent.shape[1:], 0)

    def mark_empty(j):
        val = jnp.where(slot_row < counts_ref[0, j], grad_ref[0, j].astype(f32), EMPTY)
        sent[j] = val.astype(bf16)

    chunks(data_size, mark_empty)
    own_cot = pltpu.make_async_copy(sent.at[data, :, part_cols(0, me)], cot.at[slot], own_sem.at[4])
    own_cot.start()
    clear(shifted.at[0])
    clear(att_pad)
    clear(dk)
    clear(dv)
    pl.semaphore_wait(barrier_sem, data_size * size - 1)

    def seg_copy(k):
        return remote(
            seg_ref.at[0], seg_all.at[me], seq_send.at[k - 1, 6], seq_recv.at[k - 1, 6], data, to[k]
        )

    def seq_copy(k, p, half, first, count):
        start, lanes = ((0, 2 * LANES), (2 * LANES, part - 2 * LANES))[half]
        src_col = pl.multiple_of(p * width + to[k] * part + start, LANES)
        return remote(
            qkv_ref.at[pl.ds(first, count), pl.ds(src_col, lanes)],
            mine.at[
                pl.ds(pl.multiple_of(me * rows_here + first, SLICE), count),
                pl.ds(p * part + start, lanes),
            ],
            seq_send.at[k - 1, 3 * half + p],
            seq_recv.at[k - 1, 3 * half + p],
            data,
            to[k],
        )

    def in_copy(dp, m):
        remote(
            sent.at[dp, :, part_cols(0, to[m])], cot.at[slot], in_send.at[m], in_recv.at[m], dp, to[m]
        ).start()

    for k in range(1, size):
        seg_copy(k).start()

    def begin(e):
        for k in range(1, size):
            for p in range(3):
                seq_copy(k, p, 0, pl.multiple_of(e * SLICE, SLICE), SLICE).start()
        partners(e, in_copy)

    loop(0, group, begin)
    early = group * SLICE
    for first, half in ((early, 0), (0, 1)):
        for p in range(3):
            for k in range(1, size):
                seq_copy(k, p, half, first, rows_here - first).start()

    def bytes_of(m, ref):
        got = ref.at[pl.ds(0, data_size if m else data_size - 1)]
        return got, got

    for copy in own + [own_cot]:
        copy.wait()
    for k in range(1, size):
        seg_copy(k).wait()
    for m in range(size):
        pltpu.make_async_copy(*bytes_of(m, out_ref.at[:, 0, pl.ds(0, tiles)]), in_recv.at[m]).wait()

    def cols_of(j):
        return pl.ds(pl.multiple_of(me * part + j * LANES, LANES), LANES)

    convolve(time_rows, tiles, taps, cols_of, cot, seg_all, cw_ref, seg_row, labb, shifted, grad_pad, do_t)
    def results(first, last):
        def step(c):
            here, there = rows(c, CH), rows(c, CH // slots)
            for j in range(first, last):
                cols = pl.ds(j * LANES, LANES)
                for p, val in enumerate(
                    ((dq_t[cols, here] * scale).T, dk[here, cols] * scale, dv[here, cols])
                ):
                    stage[there, p, j] = val.reshape(CH // slots, slots, LANES).astype(bf16)

        chunks(time_rows // CH, step)

    def out_pair(index, half):
        if half == 0:
            return stage.at[index, :, 0], out_ref.at[data, :, me * tiles]
        here = pl.ds(1, tiles - 1)
        return stage.at[index, :, here], out_ref.at[data, :, pl.ds(me * tiles + 1, tiles - 1)]

    def leave(half):
        def copy(dp, m):
            src, dst = out_pair(to[m] * data_size + dp, half)
            remote(src, dst, out_send.at[m, half], out_recv.at[m, half], dp, to[m]).start()

        return lambda e: partners(e, copy)

    def own_out(half):
        copy = pltpu.make_async_copy(*out_pair(slot, half), own_sem.at[half])
        copy.start()
        return copy

    for half in range(2):
        for k in range(1, size):
            for p in range(3):
                seq_copy(k, p, half, 0, rows_here).wait_recv()
        flip(time_rows, part, ((0, 1), (2,))[half], mine, k_t, v_t)
        attend(
            half * PAIR,
            time_rows,
            part,
            head_size,
            mine,
            seg_row,
            labb,
            k_t,
            v_t,
            do_t,
            att_t,
            dq_t,
            dk,
            dv,
            scores,
            probs,
        )
        if half == 0:
            results(0, 1)
            own = [own_out(0)]
            loop(0, group, leave(0))
        else:
            results(1, tiles)
            own.append(own_out(1))
            loop(0, group // 2, leave(1))

    spread_rows(
        lambda c, j: att_t[pl.ds(j * LANES, LANES), rows(c, CH)].T, labb, att_pad, time_rows, 0, tiles
    )
    inner = time_rows + GAP * (SEGMENTS - 1)
    each = terms.shape[1]
    terms[group - 1] = jnp.zeros(terms.shape[1:], f32)
    for j in range(tiles):
        cols = pl.ds(j * LANES, LANES)

        def tap_step(c, sums):
            att = att_pad[rows(c, 8), cols]
            return tuple(
                sums[w] + att * tap_view(shifted, margin, w, c * 8, 8, cols) for w in range(taps)
            )

        sums = lax.fori_loop(
            0, inner // 8, tap_step, tuple(jnp.zeros((8, LANES), f32) for _ in range(taps))
        )
        for w in range(taps):
            terms[w // each, w % each : w % each + 1, cols] = jnp.sum(sums[w], axis=0, keepdims=True)

    near_to = [lax.rem(near + k, group) for k in range(group)]
    far_to = [lax.rem(far + k, group) for k in range(group)]
    used = [0]

    def tap_copy(src, dst, z, n, m):
        i = used[0]
        used[0] += 1
        copy = remote(src, dst, tap_send.at[i], tap_recv.at[i], z * group + n, to[m])
        copy.start()
        return copy

    copies = [
        tap_copy(terms.at[near_to[k]], near_sum.at[k - 1], far, near_to[k], 0) for k in range(1, group)
    ]
    loop(group // 2, group - 2, leave(1))
    for copy in copies:
        copy.wait()
    total = terms[near]
    for k in range(1, group):
        total = total + near_sum[k - 1]
    far_sum[far] = total
    copies = [tap_copy(far_sum.at[far], far_sum.at[far], far_to[k], near, 0) for k in range(1, group)]
    loop(group - 2, group, leave(1))
    for copy in copies:
        copy.wait()
    total = far_sum[0]
    for k in range(1, group):
        total = total + far_sum[k]
    whole[me, near] = total * factor
    copies = [
        tap_copy(whole.at[me, near], whole.at[me, near], far, near_to[k], m)
        for k in range(group)
        for m in range(size)
        if k or m
    ]
    for copy in copies:
        copy.wait()
    for m in range(size):
        for g in range(group):
            count = min(each, taps - g * each)
            taps_ref[g * each : g * each + count, m * part : (m + 1) * part] = whole[m, g, :count]

    for copy in own:
        copy.wait()
    for k in range(1, size):
        for p in range(3):
            for half in range(2):
                seq_copy(k, p, half, 0, rows_here).wait_send()
    for m in range(size):
        pltpu.make_async_copy(*bytes_of(m, out_ref.at[:, 0, pl.ds(0, tiles)]), in_send.at[m]).wait()
        for half, ref in enumerate((out_ref.at[:, :, 0], out_ref.at[:, :, pl.ds(0, tiles - 1)])):
            pltpu.make_async_copy(*bytes_of(m, ref), out_send.at[m, half]).wait()
            pltpu.make_async_copy(*bytes_of(m, ref), out_recv.at[m, half]).wait()


VMEM = pl.BlockSpec(memory_space=pltpu.VMEM)
ANY = pl.BlockSpec(memory_space=pl.ANY)


def run_block(qkv, grad_in, counts, seg, cw, data_size, size, head_size, factor):
    f32, bf16 = jnp.float32, jnp.bfloat16
    _, rows_here, columns = qkv.shape
    taps = cw.shape[0]
    slots = grad_in.shape[2]
    time_rows, width = rows_here * size, columns // 3 // size
    tiles = width // LANES
    inner = -(-(time_rows + GAP * (SEGMENTS - 1)) // 96) * 96
    rows_all = inner + 48 + 8
    group = math.isqrt(data_size)
    piece = (group, (taps + 1) // group, width)
    sends = 2 * (group - 1) + group * size - 1
    dma = pltpu.SemaphoreType.DMA
    return pl.pallas_call(
        functools.partial(block_kernel, data_size, size, head_size, factor),
        out_shape=(
            jax.ShapeDtypeStruct((data_size, 3, size * tiles, slots, LANES), bf16),
            jax.ShapeDtypeStruct((taps, width * size), f32),
        ),
        in_specs=[ANY, VMEM, pl.BlockSpec(memory_space=pltpu.SMEM), ANY, VMEM],
        out_specs=(ANY, VMEM),
        scratch_shapes=[
            pltpu.VMEM((size, 1, rows_here), seg.dtype),
            pltpu.VMEM((time_rows, 3 * width), bf16),
            pltpu.VMEM((data_size, slots, size * width), bf16),
            pltpu.VMEM((data_size * size, slots, width), bf16),
            pltpu.VMEM((data_size * size, 3, tiles, slots, LANES), bf16),
            pltpu.VMEM((1, time_rows), f32),
            pltpu.VMEM((time_rows, LANES), f32),
            pltpu.VMEM((8, rows_all, width), f32),
            pltpu.VMEM((inner, width), f32),
            pltpu.VMEM((rows_all, width), f32),
            pltpu.VMEM((width, time_rows), bf16),
            pltpu.VMEM((width, time_rows), bf16),
            pltpu.VMEM((width, time_rows), f32),
            pltpu.VMEM((width, time_rows), f32),
            pltpu.VMEM((width, time_rows), f32),
            pltpu.VMEM((time_rows, width), f32),
            pltpu.VMEM((time_rows, width), f32),
            pltpu.VMEM((time_rows, PAIR * TB), f32),
            pltpu.VMEM((time_rows, PAIR * TB), bf16),
            pltpu.VMEM(piece, f32),
            pltpu.VMEM(piece, f32),
            pltpu.VMEM(piece, f32),
            pltpu.VMEM((size,) + piece, f32),
            dma((5,)),
            dma((size - 1, 7)),
            dma((size - 1, 7)),
            dma((size,)),
            dma((size,)),
            dma((size, 2)),
            dma((size, 2)),
            dma((sends,)),
            dma((sends,)),
        ],
        compiler_params=pltpu.CompilerParams(
            collective_id=1, has_side_effects=True, vmem_limit_bytes=58 * 1024 * 1024
        ),
        cost_estimate=pl.CostEstimate(
            flops=14 * time_rows * time_rows * width, bytes_accessed=64 << 20, transcendentals=0
        ),
    )(qkv, grad_in, counts, seg[None], cw)


def local(qkv, grad_in, counts, segment, conv_weight):
    data_size = lax.axis_size("dp")
    time_size = lax.axis_size("seq")
    width = qkv.shape[2] // 3
    head_size = width // H
    slot_rows = grad_in.shape[2]

    factor = 1.0 / math.sqrt(data_size * slot_rows)
    grads, conv_weight_grad = run_block(
        qkv, grad_in, counts, segment, conv_weight, data_size, time_size, head_size, factor
    )
    qkv_grad = grads.transpose(0, 3, 1, 2, 4).reshape(1, data_size, slot_rows, 3 * width)
    return (qkv_grad, conv_weight_grad)


def solution(mesh):
    in_specs = (
        P("dp", "seq", None),
        P("dp", "seq", None, None),
        P("dp", "seq"),
        P("dp", "seq"),
        P(),
    )
    out_specs = (P("dp", "seq", None, None), P())
    return jax.shard_map(local, mesh=mesh, in_specs=in_specs, out_specs=out_specs, check_vma=False)
```

```python
import functools
import math

import jax
import jax.numpy as jnp
from jax import lax
from jax.experimental import pallas as pl
from jax.experimental.pallas import tpu as pltpu
from jax.sharding import PartitionSpec as P

H = 16

EMPTY = 128.0
EMPTY_ABOVE = 64.0
MASKED = -1e30
LANES = 128
TB = 512
UB = 256
SLICE = 16
CONV = 64
PAIR = 2
GAP = 16
SEGMENTS = 4
MESH = pl.DeviceIdType.MESH
CH = 128


def dot(a, b, contract):
    return lax.dot_general(a, b, (contract, ((), ())), preferred_element_type=jnp.float32)


def rows(index, size):
    return pl.ds(pl.multiple_of(index * size, size), size)


def chunks(count, body):
    def step(index, carry):
        body(index)
        return carry

    lax.fori_loop(0, count, step, 0)


def tap_view(shifted, margin, w, r0, size, cols):
    offset = margin - w
    a, b = offset // 8, offset % 8
    return shifted[b, pl.ds(pl.multiple_of(r0 + GAP + 8 * a, 8), size), cols]


def clear(ref):
    def step(c):
        ref[rows(c, 8), :] = jnp.zeros((8, ref.shape[1]), ref.dtype)

    chunks(ref.shape[0] // 8, step)


def spread_rows(value, labb, target, time_rows, shift, tiles):
    def step(c):
        lab = labb[rows(c, CH), :]
        for j in tiles:
            val = value(c, j)
            for s in range(SEGMENTS):
                there = pl.ds(pl.multiple_of(c * CH + GAP * (s + shift), GAP), CH)
                target[there, pl.ds(j * LANES, LANES)] += jnp.where(lab == s + 1.0, val, 0.0)

    chunks(time_rows // CH, step)


def label_rows(time_rows, cot_rows, seg_ref, seg_row, labb):
    piece = seg_ref.shape[2]
    for s in range(seg_ref.shape[0]):
        seg_row[:, s * piece : (s + 1) * piece] = seg_ref[s].astype(jnp.float32)

    def label(c):
        here = rows(c, CH)
        across = jnp.broadcast_to(seg_row[:, here], (CH, CH)).T
        labb[here, :] = jnp.where(cot_rows(c, 0) < EMPTY_ABOVE, across + 1.0, 0.0)

    chunks(time_rows // CH, label)


def convolve(time_rows, tiles, taps, cols_of, cot_rows, cw_ref, labb, shifted, grad_pad, do_t):
    f32 = jnp.float32
    margin = (taps - 1) // 2
    spread_rows(cot_rows, labb, shifted.at[0], time_rows, 1, tiles)

    def shift(c):
        r0 = pl.multiple_of(c * 48, 8)
        for j in tiles:
            cols = pl.ds(j * LANES, LANES)
            block = shifted[0, pl.ds(r0, 56), cols]
            for b in range(1, 8):
                shifted[b, pl.ds(r0, 48), cols] = block[b : b + 48]

    chunks((shifted.shape[1] - 8) // 48, shift)

    def conv(c):
        r0 = pl.multiple_of(c * CONV, CONV)
        for j in tiles:
            cols = pl.ds(j * LANES, LANES)
            total = jnp.zeros((CONV, LANES), f32)
            for b in range(8):
                block = shifted[b, pl.ds(r0, CONV + 2 * GAP - 8), cols]
                for a in range(-2, 2):
                    w = margin - 8 * a - b
                    if 0 <= w < taps:
                        weight = cw_ref[w : w + 1, cols_of(j)]
                        total = total + weight * block[GAP + 8 * a : GAP + 8 * a + CONV]
            grad_pad[pl.ds(r0, CONV), cols] = total

    chunks(grad_pad.shape[0] // CONV, conv)

    def collect(c):
        lab = labb[rows(c, CH), :]
        for j in tiles:
            cols = pl.ds(j * LANES, LANES)
            total = jnp.zeros((CH, LANES), f32)
            for s in range(SEGMENTS):
                there = pl.ds(pl.multiple_of(c * CH + GAP * s, GAP), CH)
                total = total + jnp.where(lab == s + 1.0, grad_pad[there, cols], 0.0)
            do_t[cols, rows(c, CH)] = total.astype(jnp.bfloat16).T

    chunks(time_rows // CH, collect)


def flip(time_rows, width, tiles, qkv_ref, k_t, v_t):
    def step(c):
        here = rows(c, CH)
        for j in tiles:
            for n, target in ((1, k_t), (2, v_t)):
                block = qkv_ref[here, pl.ds(n * width + j * LANES, LANES)]
                target[pl.ds(j * LANES, LANES), here] = block.T

    chunks(time_rows // CH, step)


def attend(
    h0, time_rows, width, head_size, qkv_ref, seg_row, labb, k_t, v_t, do_t, att_t, dq_t, dk, dv, scores, probs
):
    f32, bf16 = jnp.float32, jnp.bfloat16
    scale = head_size ** (-0.5)
    cols_here = PAIR * TB
    row_index = lax.broadcasted_iota(jnp.int32, (UB, cols_here), 0)
    col_index = lax.broadcasted_iota(jnp.int32, (UB, cols_here), 1) % TB
    apart = col_index - row_index
    to_exp2 = scale * math.log2(math.e)

    first, last = h0 * head_size, (h0 + PAIR) * head_size
    lane0 = first // LANES * LANES
    span = -(-last // LANES) * LANES - lane0
    lane = lax.broadcasted_iota(jnp.int32, (TB, span), 1) + lane0
    head_rows = [pl.ds((h0 + n) * head_size, head_size) for n in range(PAIR)]

    def beside(values):
        return jnp.concatenate(values, axis=1)

    def time_block(tb, carry):
        here = rows(tb, TB)
        q = qkv_ref[here, pl.ds(lane0, span)]
        q = jnp.concatenate(
            [
                jnp.where(
                    (lane >= (h0 + n) * head_size) & (lane < (h0 + n + 1) * head_size),
                    q,
                    jnp.zeros((), bf16),
                )
                for n in range(PAIR)
            ],
            axis=0,
        )
        want = beside([seg_row[:, here] + 1.0] * PAIR)

        def score_step(ub, highest):
            keys = rows(ub, UB)
            s = dot(qkv_ref[keys, pl.ds(width + lane0, span)], q, ((1,), (1,)))
            lab = beside([labb[keys, :]] * (cols_here // LANES))
            ok = (lab == want) | (apart == ub * UB - tb * TB)
            s = jnp.where(ok, s, MASKED)
            scores[keys, :] = s
            return jnp.maximum(highest, jnp.max(s.reshape(UB // 8, 8, cols_here), axis=0))

        highest = lax.fori_loop(0, time_rows // UB, score_step, jnp.full((8, cols_here), MASKED, f32), unroll=True)
        highest = jnp.max(highest, axis=0, keepdims=True) * to_exp2
        for n in range(PAIR):
            att_t[head_rows[n], here] = jnp.zeros((head_size, TB), f32)
            dq_t[head_rows[n], here] = jnp.zeros((head_size, TB), f32)

        def soft_step(ub, total):
            keys = rows(ub, UB)
            p = jnp.exp2(scores[keys, :] * to_exp2 - highest)
            total = total + jnp.sum(p.reshape(UB // 8, 8, cols_here), axis=0)
            p = p.astype(bf16)
            probs[keys, :] = p
            for n in range(PAIR):
                att_t[head_rows[n], here] += dot(
                    v_t[head_rows[n], keys], p[:, n * TB : (n + 1) * TB], ((1,), (0,))
                )
            return total

        total = lax.fori_loop(0, time_rows // UB, soft_step, jnp.zeros((8, cols_here), f32), unroll=True)
        inverse = 1.0 / jnp.sum(total, axis=0, keepdims=True)
        deltas, wide = [], []
        for n in range(PAIR):
            inv = inverse[:, n * TB : (n + 1) * TB]
            att = (att_t[head_rows[n], here] * inv).astype(bf16).astype(f32)
            att_t[head_rows[n], here] = att
            do = do_t[head_rows[n], here].astype(f32)
            deltas.append(jnp.sum(do * att, axis=0, keepdims=True) * inv)
            before = (h0 + n) * head_size - lane0
            after = span - before - head_size
            parts = [(do * inv).astype(bf16)]
            if before:
                parts = [jnp.zeros((before, TB), bf16)] + parts
            if after:
                parts = parts + [jnp.zeros((after, TB), bf16)]
            wide.append(jnp.concatenate(parts, axis=0))
        delta, do_wide = beside(deltas), beside(wide)

        def grad_step(ub, carry):
            keys = rows(ub, UB)
            p = probs[keys, :]
            dp = dot(qkv_ref[keys, pl.ds(2 * width + lane0, span)], do_wide, ((1,), (0,)))
            ds = (p.astype(f32) * (dp - delta)).astype(bf16)
            dk[keys, pl.ds(lane0, span)] += dot(ds, q, ((1,), (0,)))
            dv[keys, pl.ds(lane0, span)] += dot(p, do_wide, ((1,), (1,)))
            for n in range(PAIR):
                dq_t[head_rows[n], here] += dot(
                    k_t[head_rows[n], keys], ds[:, n * TB : (n + 1) * TB], ((1,), (0,))
                )
            return carry

        lax.fori_loop(0, time_rows // UB, grad_step, 0, unroll=True)
        return carry

    lax.fori_loop(0, time_rows // TB, time_block, 0)


def block_kernel(
    data_size,
    size,
    head_size,
    factor,
    qkv_ref,
    grad_in_ref,
    counts_ref,
    seg_ref,
    weights_ref,
    out_ref,
    taps_ref,
    seg_all,
    mine,
    grad_ref,
    cw_ref,
    sent,
    cot,
    stage,
    seg_row,
    labb,
    shifted,
    grad_pad,
    att_pad,
    k_t,
    v_t,
    do_t,
    att_t,
    dq_t,
    dk,
    dv,
    scores,
    probs,
    terms,
    near_sum,
    far_sum,
    whole,
    all_in,
    own_sem,
    seq_send,
    seq_recv,
    in_send,
    in_recv,
    out_send,
    out_recv,
    tap_send,
    tap_recv,
):
    f32, bf16 = jnp.float32, jnp.bfloat16
    data, me = lax.axis_index("dp"), lax.axis_index("seq")
    group = math.isqrt(data_size)
    far, near = data // group, lax.rem(data, group)
    qkv_ref = qkv_ref.at[0]
    rows_here = qkv_ref.shape[0]
    time_rows = rows_here * size
    taps = cw_ref.shape[0]
    margin = (taps - 1) // 2
    part = qkv_ref.shape[1] // 3 // size
    width = part * size
    tiles = part // LANES
    slots = cot.shape[1]
    scale = head_size ** (-0.5)
    to = [lax.rem(me + k, size) for k in range(size)]
    far_order = [0]
    for k in range(1, group // 2 + 1):
        far_order = ([k, group - k] if 2 * k < group else [k]) + far_order

    def partners(e, body):
        for m in range(size):
            for z in far_order:
                if z or m:
                    body(lax.rem(far + z, group) * group + lax.rem(near + e, group), m)

    def neighbours(body):
        for k in range(1, group):
            body(far * group + lax.rem(near + k, group), 0)

    def loop(first, last, body):
        def step(e, carry):
            body(e)
            return carry

        lax.fori_loop(first, last, step, 0)

    def remote(src, dst, send, recv, dp, seq):
        return pltpu.make_async_remote_copy(
            src_ref=src,
            dst_ref=dst,
            send_sem=send,
            recv_sem=recv,
            device_id={"dp": dp, "seq": seq},
            device_id_type=MESH,
        )

    barrier_sem = pltpu.get_barrier_semaphore()

    def greet(dp, m):
        pl.semaphore_signal(
            barrier_sem, inc=1, device_id={"dp": dp, "seq": to[m]}, device_id_type=MESH
        )

    across = [(z, m) for z in range(group) for m in range(size) if z or m]
    neighbours(greet)
    for z, m in across:
        greet(lax.rem(far + z, group) * group + near, m)

    def part_cols(p, d):
        return pl.ds(pl.multiple_of(p * width + d * part, part), part)

    slot = me * data_size + data
    grad_copy = pltpu.make_async_copy(grad_in_ref, grad_ref, own_sem.at[5])
    grad_copy.start()
    moves = [(seg_ref.at[0], seg_all.at[me])]
    for p in range(3):
        moves.append(
            (qkv_ref.at[:, part_cols(p, me)], mine.at[rows(me, rows_here), pl.ds(p * part, part)])
        )
    moves.append((weights_ref, cw_ref))
    own = [pltpu.make_async_copy(src, dst, own_sem.at[n]) for n, (src, dst) in enumerate(moves)]
    for copy in own:
        copy.start()
    grad_copy.wait()
    slot_row = lax.broadcasted_iota(jnp.int32, sent.shape[1:], 0)

    def mark_empty(j):
        val = jnp.where(slot_row < counts_ref[0, j], grad_ref[0, j].astype(f32), EMPTY)
        sent[j] = val.astype(bf16)

    chunks(data_size, mark_empty)
    own_cot = pltpu.make_async_copy(sent.at[data, :, part_cols(0, me)], cot.at[slot], own_sem.at[6])
    own_cot.start()
    clear(shifted.at[0])
    clear(att_pad)
    clear(dk)
    clear(dv)
    pl.semaphore_wait(barrier_sem, group - 1 + len(across))
    for z, m in across:
        pl.semaphore_signal(
            all_in,
            inc=1,
            device_id={"dp": lax.rem(far + z, group) * group + near, "seq": to[m]},
            device_id_type=MESH,
        )

    halves = ((0, 2 * LANES), (2 * LANES, part - 2 * LANES))

    def seg_copy(k):
        return remote(
            seg_ref.at[0], seg_all.at[me], seq_send.at[k - 1, 6], seq_recv.at[k - 1, 6], data, to[k]
        )

    def seq_copy(k, p, half, first, count):
        start, lanes = halves[half]
        src_col = pl.multiple_of(p * width + to[k] * part + start, LANES)
        return remote(
            qkv_ref.at[pl.ds(first, count), pl.ds(src_col, lanes)],
            mine.at[
                pl.ds(pl.multiple_of(me * rows_here + first, SLICE), count),
                pl.ds(p * part + start, lanes),
            ],
            seq_send.at[k - 1, 3 * half + p],
            seq_recv.at[k - 1, 3 * half + p],
            data,
            to[k],
        )

    def in_copy(half):
        start, lanes = halves[half]

        def copy(dp, m):
            src_col = pl.multiple_of(to[m] * part + start, LANES)
            remote(
                sent.at[dp, :, pl.ds(src_col, lanes)],
                cot.at[slot, :, pl.ds(start, lanes)],
                in_send.at[m, half],
                in_recv.at[m, half],
                dp,
                to[m],
            ).start()

        return copy

    for k in range(1, size):
        seg_copy(k).start()

    pl.semaphore_wait(all_in, len(across))

    def begin(half, slice_rows):
        def step(e):
            for k in range(1, size):
                for p in range(3):
                    first = pl.multiple_of(e * slice_rows, slice_rows)
                    seq_copy(k, p, half, first, slice_rows).start()
            partners(e, in_copy(half))

        loop(0, group, step)
        neighbours(in_copy(half))

    begin(0, SLICE)
    early = group * SLICE
    for p in range(3):
        for k in range(1, size):
            seq_copy(k, p, 0, early, rows_here - early).start()

    def bytes_of(m, ref):
        got = ref.at[pl.ds(0, data_size if m else data_size - 1)]
        return got, got

    for copy in own + [own_cot]:
        copy.wait()
    for k in range(1, size):
        seg_copy(k).wait()
    def in_bytes(m, half):
        return bytes_of(m, out_ref.at[:, 0, pl.ds(0, halves[half][1] // LANES)])

    def cols_of(j):
        return pl.ds(pl.multiple_of(me * part + j * LANES, LANES), LANES)

    def cot_rows(c, j):
        val = cot[rows(c, CH // slots), :, pl.ds(j * LANES, LANES)].astype(f32)
        return val.reshape(CH, LANES)

    def results(first, last):
        def step(c):
            here, there = rows(c, CH), rows(c, CH // slots)
            for j in range(first, last):
                cols = pl.ds(j * LANES, LANES)
                for p, val in enumerate(
                    ((dq_t[cols, here] * scale).T, dk[here, cols] * scale, dv[here, cols])
                ):
                    stage[there, p, j] = val.reshape(CH // slots, slots, LANES).astype(bf16)

        chunks(time_rows // CH, step)

    def out_pair(index, half):
        if half == 0:
            return stage.at[index, :, 0], out_ref.at[data, :, me * tiles]
        here = pl.ds(1, tiles - 1)
        return stage.at[index, :, here], out_ref.at[data, :, pl.ds(me * tiles + 1, tiles - 1)]

    def leave(half):
        def copy(dp, m):
            src, dst = out_pair(to[m] * data_size + dp, half)
            remote(src, dst, out_send.at[m, half], out_recv.at[m, half], dp, to[m]).start()

        return copy, lambda e: partners(e, copy)

    def own_out(half):
        copy = pltpu.make_async_copy(*out_pair(slot, half), own_sem.at[half])
        copy.start()
        return copy

    for half in range(2):
        new = ((0, 1), (2,))[half]
        for m in range(size):
            pltpu.make_async_copy(*in_bytes(m, half), in_recv.at[m, half]).wait()
        if half == 0:
            label_rows(time_rows, cot_rows, seg_all, seg_row, labb)
        convolve(time_rows, new, taps, cols_of, cot_rows, cw_ref, labb, shifted, grad_pad, do_t)
        for k in range(1, size):
            for p in range(3):
                seq_copy(k, p, half, 0, rows_here).wait_recv()
        if half == 0:
            begin(1, rows_here // group)
        flip(time_rows, part, new, mine, k_t, v_t)
        attend(
            half * PAIR,
            time_rows,
            part,
            head_size,
            mine,
            seg_row,
            labb,
            k_t,
            v_t,
            do_t,
            att_t,
            dq_t,
            dk,
            dv,
            scores,
            probs,
        )
        if half == 0:
            results(0, 1)
            own = [own_out(0)]
            neighbours(leave(0)[0])
            loop(0, group, leave(0)[1])
        else:
            results(1, tiles)
            own.append(own_out(1))
            neighbours(leave(1)[0])
            loop(0, group // 2, leave(1)[1])

    spread_rows(
        lambda c, j: att_t[pl.ds(j * LANES, LANES), rows(c, CH)].T, labb, att_pad, time_rows, 0, range(tiles)
    )
    inner = time_rows + GAP * (SEGMENTS - 1)
    each = terms.shape[1]
    terms[group - 1] = jnp.zeros(terms.shape[1:], f32)
    for j in range(tiles):
        cols = pl.ds(j * LANES, LANES)

        def tap_step(c, sums):
            att = att_pad[rows(c, 8), cols]
            return tuple(
                sums[w] + att * tap_view(shifted, margin, w, c * 8, 8, cols) for w in range(taps)
            )

        sums = lax.fori_loop(
            0, inner // 8, tap_step, tuple(jnp.zeros((8, LANES), f32) for _ in range(taps))
        )
        for w in range(taps):
            terms[w // each, w % each : w % each + 1, cols] = jnp.sum(sums[w], axis=0, keepdims=True)

    near_to = [lax.rem(near + k, group) for k in range(group)]
    far_to = [lax.rem(far + k, group) for k in range(group)]
    used = [0]

    def tap_copy(src, dst, z, n, m):
        i = used[0]
        used[0] += 1
        copy = remote(src, dst, tap_send.at[i], tap_recv.at[i], z * group + n, to[m])
        copy.start()
        return copy

    copies = [
        tap_copy(terms.at[near_to[k]], near_sum.at[k - 1], far, near_to[k], 0) for k in range(1, group)
    ]
    loop(group // 2, group - 2, leave(1)[1])
    for copy in copies:
        copy.wait()
    total = terms[near]
    for k in range(1, group):
        total = total + near_sum[k - 1]
    far_sum[far] = total
    copies = [tap_copy(far_sum.at[far], far_sum.at[far], far_to[k], near, 0) for k in range(1, group)]
    loop(group - 2, group, leave(1)[1])
    for copy in copies:
        copy.wait()
    total = far_sum[0]
    for k in range(1, group):
        total = total + far_sum[k]
    whole[me, near] = total * factor
    copies = [
        tap_copy(whole.at[me, near], whole.at[me, near], far, near_to[k], m)
        for k in range(group)
        for m in range(size)
        if k or m
    ]
    for copy in copies:
        copy.wait()
    for m in range(size):
        for g in range(group):
            count = min(each, taps - g * each)
            taps_ref[g * each : g * each + count, m * part : (m + 1) * part] = whole[m, g, :count]

    for copy in own:
        copy.wait()
    for k in range(1, size):
        for p in range(3):
            for half in range(2):
                seq_copy(k, p, half, 0, rows_here).wait_send()
    for m in range(size):
        for half in range(2):
            pltpu.make_async_copy(*in_bytes(m, half), in_send.at[m, half]).wait()
        for half, ref in enumerate((out_ref.at[:, :, 0], out_ref.at[:, :, pl.ds(0, tiles - 1)])):
            pltpu.make_async_copy(*bytes_of(m, ref), out_send.at[m, half]).wait()
            pltpu.make_async_copy(*bytes_of(m, ref), out_recv.at[m, half]).wait()


VMEM = pl.BlockSpec(memory_space=pltpu.VMEM)
ANY = pl.BlockSpec(memory_space=pl.ANY)


def run_block(qkv, grad_in, counts, seg, cw, data_size, size, head_size, factor):
    f32, bf16 = jnp.float32, jnp.bfloat16
    _, rows_here, columns = qkv.shape
    taps = cw.shape[0]
    slots = grad_in.shape[2]
    time_rows, width = rows_here * size, columns // 3 // size
    tiles = width // LANES
    inner = -(-(time_rows + GAP * (SEGMENTS - 1)) // CONV) * CONV
    rows_all = -(-(inner + 2 * GAP) // 48) * 48 + 8
    group = math.isqrt(data_size)
    piece = (group, (taps + 1) // group, width)
    sends = 2 * (group - 1) + group * size - 1
    dma = pltpu.SemaphoreType.DMA
    return pl.pallas_call(
        functools.partial(block_kernel, data_size, size, head_size, factor),
        out_shape=(
            jax.ShapeDtypeStruct((data_size, 3, size * tiles, slots, LANES), bf16),
            jax.ShapeDtypeStruct((taps, width * size), f32),
        ),
        in_specs=[ANY, ANY, pl.BlockSpec(memory_space=pltpu.SMEM), ANY, ANY],
        out_specs=(ANY, VMEM),
        scratch_shapes=[
            pltpu.VMEM((size, 1, rows_here), seg.dtype),
            pltpu.VMEM((time_rows, 3 * width), bf16),
            pltpu.VMEM((1, data_size, slots, size * width), bf16),
            pltpu.VMEM(cw.shape, f32),
            pltpu.VMEM((data_size, slots, size * width), bf16),
            pltpu.VMEM((data_size * size, slots, width), bf16),
            pltpu.VMEM((data_size * size, 3, tiles, slots, LANES), bf16),
            pltpu.VMEM((1, time_rows), f32),
            pltpu.VMEM((time_rows, LANES), f32),
            pltpu.VMEM((8, rows_all, width), f32),
            pltpu.VMEM((inner, width), f32),
            pltpu.VMEM((rows_all, width), f32),
            pltpu.VMEM((width, time_rows), bf16),
            pltpu.VMEM((width, time_rows), bf16),
            pltpu.VMEM((width, time_rows), bf16),
            pltpu.VMEM((width, time_rows), f32),
            pltpu.VMEM((width, time_rows), f32),
            pltpu.VMEM((time_rows, width), f32),
            pltpu.VMEM((time_rows, width), f32),
            pltpu.VMEM((time_rows, PAIR * TB), f32),
            pltpu.VMEM((time_rows, PAIR * TB), bf16),
            pltpu.VMEM(piece, f32),
            pltpu.VMEM(piece, f32),
            pltpu.VMEM(piece, f32),
            pltpu.VMEM((size,) + piece, f32),
            pltpu.SemaphoreType.REGULAR,
            dma((7,)),
            dma((size - 1, 7)),
            dma((size - 1, 7)),
            dma((size, 2)),
            dma((size, 2)),
            dma((size, 2)),
            dma((size, 2)),
            dma((sends,)),
            dma((sends,)),
        ],
        compiler_params=pltpu.CompilerParams(
            collective_id=1, has_side_effects=True, vmem_limit_bytes=58 * 1024 * 1024
        ),
        cost_estimate=pl.CostEstimate(
            flops=14 * time_rows * time_rows * width, bytes_accessed=64 << 20, transcendentals=0
        ),
    )(qkv, grad_in, counts, seg[None], cw)


def hand_on_kernel(grads_ref, taps_ref, grads_out, taps_out, held, came, left):
    pieces = came.shape[0]
    count = held.shape[0] // pieces
    here = [pl.ds(n * count, count) for n in range(pieces)]
    reads = [pltpu.make_async_copy(grads_ref.at[h], held.at[h], came.at[n]) for n, h in enumerate(here)]
    writes = [pltpu.make_async_copy(held.at[h], grads_out.at[h], left.at[n]) for n, h in enumerate(here)]
    for copy in reads:
        copy.start()
    taps_out[...] = taps_ref[...]
    for n in range(pieces):
        reads[n].wait()
        writes[n].start()
    for copy in writes:
        copy.wait()


def hand_on(grads, total):
    return pl.pallas_call(
        hand_on_kernel,
        out_shape=tuple(jax.ShapeDtypeStruct(x.shape, x.dtype) for x in (grads, total)),
        in_specs=[ANY, VMEM],
        out_specs=(ANY, VMEM),
        scratch_shapes=[
            pltpu.VMEM(grads.shape, grads.dtype),
            pltpu.SemaphoreType.DMA((8,)),
            pltpu.SemaphoreType.DMA((8,)),
        ],
        compiler_params=pltpu.CompilerParams(vmem_limit_bytes=60 * 1024 * 1024),
    )(grads, total)


def local(qkv, grad_in, counts, segment, conv_weight):
    data_size = lax.axis_size("dp")
    time_size = lax.axis_size("seq")
    width = qkv.shape[2] // 3
    head_size = width // H
    slot_rows = grad_in.shape[2]

    factor = 1.0 / math.sqrt(data_size * slot_rows)
    grads, conv_weight_grad = run_block(
        qkv, grad_in, counts, segment, conv_weight, data_size, time_size, head_size, factor
    )
    grads, conv_weight_grad = hand_on(grads, conv_weight_grad)
    qkv_grad = grads.transpose(0, 3, 1, 2, 4).reshape(1, data_size, slot_rows, 3 * width)
    return (qkv_grad, conv_weight_grad)


def solution(mesh):
    in_specs = (
        P("dp", "seq", None),
        P("dp", "seq", None, None),
        P("dp", "seq"),
        P("dp", "seq"),
        P(),
    )
    out_specs = (P("dp", "seq", None, None), P())
    return jax.shard_map(local, mesh=mesh, in_specs=in_specs, out_specs=out_specs, check_vma=False)
```

```python
import functools
import math

import jax
import jax.numpy as jnp
from jax import lax
from jax.experimental import pallas as pl
from jax.experimental.pallas import tpu as pltpu
from jax.sharding import PartitionSpec as P

H = 16

EMPTY = 128.0
EMPTY_ABOVE = 64.0
MASKED = -1e30
LANES = 128
TB = 512
UB = 256
SLICE = 16
CONV = 64
PAIR = 2
GAP = 16
SEGMENTS = 4
MESH = pl.DeviceIdType.MESH
CH = 128


def dot(a, b, contract):
    return lax.dot_general(a, b, (contract, ((), ())), preferred_element_type=jnp.float32)


def rows(index, size):
    return pl.ds(pl.multiple_of(index * size, size), size)


def chunks(count, body):
    def step(index, carry):
        body(index)
        return carry

    lax.fori_loop(0, count, step, 0)


def tap_view(shifted, margin, w, r0, size, cols):
    offset = margin - w
    a, b = offset // 8, offset % 8
    return shifted[b, pl.ds(pl.multiple_of(r0 + GAP + 8 * a, 8), size), cols]


def clear(ref):
    def step(c):
        ref[rows(c, 8), :] = jnp.zeros((8, ref.shape[1]), ref.dtype)

    chunks(ref.shape[0] // 8, step)


def spread_rows(value, labb, target, time_rows, shift, tiles):
    def step(c):
        lab = labb[rows(c, CH), :]
        for j in tiles:
            val = value(c, j)
            for s in range(SEGMENTS):
                there = pl.ds(pl.multiple_of(c * CH + GAP * (s + shift), GAP), CH)
                target[there, pl.ds(j * LANES, LANES)] += jnp.where(lab == s + 1.0, val, 0.0)

    chunks(time_rows // CH, step)


def label_rows(time_rows, cot_rows, seg_ref, seg_row, labb):
    piece = seg_ref.shape[2]
    for s in range(seg_ref.shape[0]):
        seg_row[:, s * piece : (s + 1) * piece] = seg_ref[s].astype(jnp.float32)

    def label(c):
        here = rows(c, CH)
        across = jnp.broadcast_to(seg_row[:, here], (CH, CH)).T
        labb[here, :] = jnp.where(cot_rows(c, 0) < EMPTY_ABOVE, across + 1.0, 0.0)

    chunks(time_rows // CH, label)


def convolve(time_rows, tiles, taps, cols_of, cot_rows, cw_ref, labb, shifted, grad_pad, do_t):
    f32 = jnp.float32
    margin = (taps - 1) // 2
    spread_rows(cot_rows, labb, shifted.at[0], time_rows, 1, tiles)

    def shift(c):
        r0 = pl.multiple_of(c * 48, 8)
        for j in tiles:
            cols = pl.ds(j * LANES, LANES)
            block = shifted[0, pl.ds(r0, 56), cols]
            for b in range(1, 8):
                shifted[b, pl.ds(r0, 48), cols] = block[b : b + 48]

    chunks((shifted.shape[1] - 8) // 48, shift)

    def conv(c):
        r0 = pl.multiple_of(c * CONV, CONV)
        for j in tiles:
            cols = pl.ds(j * LANES, LANES)
            total = jnp.zeros((CONV, LANES), f32)
            for b in range(8):
                block = shifted[b, pl.ds(r0, CONV + 2 * GAP - 8), cols]
                for a in range(-2, 2):
                    w = margin - 8 * a - b
                    if 0 <= w < taps:
                        weight = cw_ref[w : w + 1, cols_of(j)]
                        total = total + weight * block[GAP + 8 * a : GAP + 8 * a + CONV]
            grad_pad[pl.ds(r0, CONV), cols] = total

    chunks(grad_pad.shape[0] // CONV, conv)

    def collect(c):
        lab = labb[rows(c, CH), :]
        for j in tiles:
            cols = pl.ds(j * LANES, LANES)
            total = jnp.zeros((CH, LANES), f32)
            for s in range(SEGMENTS):
                there = pl.ds(pl.multiple_of(c * CH + GAP * s, GAP), CH)
                total = total + jnp.where(lab == s + 1.0, grad_pad[there, cols], 0.0)
            do_t[cols, rows(c, CH)] = total.astype(jnp.bfloat16).T

    chunks(time_rows // CH, collect)


def flip(time_rows, width, tiles, qkv_ref, k_t, v_t):
    def step(c):
        here = rows(c, CH)
        for j in tiles:
            for n, target in ((1, k_t), (2, v_t)):
                block = qkv_ref[here, pl.ds(n * width + j * LANES, LANES)]
                target[pl.ds(j * LANES, LANES), here] = block.T

    chunks(time_rows // CH, step)


def attend(
    h0, time_rows, width, head_size, qkv_ref, seg_row, labb, k_t, v_t, do_t, att_t, dq_t, dk, dv, scores, probs
):
    f32, bf16 = jnp.float32, jnp.bfloat16
    scale = head_size ** (-0.5)
    cols_here = PAIR * TB
    row_index = lax.broadcasted_iota(jnp.int32, (UB, cols_here), 0)
    col_index = lax.broadcasted_iota(jnp.int32, (UB, cols_here), 1) % TB
    apart = col_index - row_index
    to_exp2 = scale * math.log2(math.e)

    first, last = h0 * head_size, (h0 + PAIR) * head_size
    lane0 = first // LANES * LANES
    span = -(-last // LANES) * LANES - lane0
    lane = lax.broadcasted_iota(jnp.int32, (TB, span), 1) + lane0
    head_rows = [pl.ds((h0 + n) * head_size, head_size) for n in range(PAIR)]

    def beside(values):
        return jnp.concatenate(values, axis=1)

    def time_block(tb, carry):
        here = rows(tb, TB)
        q = qkv_ref[here, pl.ds(lane0, span)]
        q = jnp.concatenate(
            [
                jnp.where(
                    (lane >= (h0 + n) * head_size) & (lane < (h0 + n + 1) * head_size),
                    q,
                    jnp.zeros((), bf16),
                )
                for n in range(PAIR)
            ],
            axis=0,
        )
        want = beside([seg_row[:, here] + 1.0] * PAIR)

        def score_step(ub, highest):
            keys = rows(ub, UB)
            s = dot(qkv_ref[keys, pl.ds(width + lane0, span)], q, ((1,), (1,)))
            lab = beside([labb[keys, :]] * (cols_here // LANES))
            ok = (lab == want) | (apart == ub * UB - tb * TB)
            s = jnp.where(ok, s, MASKED)
            scores[keys, :] = s
            return jnp.maximum(highest, jnp.max(s.reshape(UB // 8, 8, cols_here), axis=0))

        highest = lax.fori_loop(0, time_rows // UB, score_step, jnp.full((8, cols_here), MASKED, f32), unroll=True)
        highest = jnp.max(highest, axis=0, keepdims=True) * to_exp2
        for n in range(PAIR):
            att_t[head_rows[n], here] = jnp.zeros((head_size, TB), f32)
            dq_t[head_rows[n], here] = jnp.zeros((head_size, TB), f32)

        def soft_step(ub, total):
            keys = rows(ub, UB)
            p = jnp.exp2(scores[keys, :] * to_exp2 - highest)
            total = total + jnp.sum(p.reshape(UB // 8, 8, cols_here), axis=0)
            p = p.astype(bf16)
            probs[keys, :] = p
            for n in range(PAIR):
                att_t[head_rows[n], here] += dot(
                    v_t[head_rows[n], keys], p[:, n * TB : (n + 1) * TB], ((1,), (0,))
                )
            return total

        total = lax.fori_loop(0, time_rows // UB, soft_step, jnp.zeros((8, cols_here), f32), unroll=True)
        inverse = 1.0 / jnp.sum(total, axis=0, keepdims=True)
        deltas, wide = [], []
        for n in range(PAIR):
            inv = inverse[:, n * TB : (n + 1) * TB]
            att = (att_t[head_rows[n], here] * inv).astype(bf16).astype(f32)
            att_t[head_rows[n], here] = att
            do = do_t[head_rows[n], here].astype(f32)
            deltas.append(jnp.sum(do * att, axis=0, keepdims=True) * inv)
            before = (h0 + n) * head_size - lane0
            after = span - before - head_size
            parts = [(do * inv).astype(bf16)]
            if before:
                parts = [jnp.zeros((before, TB), bf16)] + parts
            if after:
                parts = parts + [jnp.zeros((after, TB), bf16)]
            wide.append(jnp.concatenate(parts, axis=0))
        delta, do_wide = beside(deltas), beside(wide)

        def grad_step(ub, carry):
            keys = rows(ub, UB)
            p = probs[keys, :]
            dp = dot(qkv_ref[keys, pl.ds(2 * width + lane0, span)], do_wide, ((1,), (0,)))
            ds = (p.astype(f32) * (dp - delta)).astype(bf16)
            dk[keys, pl.ds(lane0, span)] += dot(ds, q, ((1,), (0,)))
            dv[keys, pl.ds(lane0, span)] += dot(p, do_wide, ((1,), (1,)))
            for n in range(PAIR):
                dq_t[head_rows[n], here] += dot(
                    k_t[head_rows[n], keys], ds[:, n * TB : (n + 1) * TB], ((1,), (0,))
                )
            return carry

        lax.fori_loop(0, time_rows // UB, grad_step, 0, unroll=True)
        return carry

    lax.fori_loop(0, time_rows // TB, time_block, 0, unroll=True)


def block_kernel(
    data_size,
    size,
    head_size,
    factor,
    qkv_ref,
    grad_in_ref,
    counts_in_ref,
    seg_ref,
    weights_ref,
    out_ref,
    taps_ref,
    seg_all,
    mine,
    grad_ref,
    counts_ref,
    cw_ref,
    sent,
    cot,
    stage,
    seg_row,
    labb,
    shifted,
    grad_pad,
    att_pad,
    k_t,
    v_t,
    do_t,
    att_t,
    dq_t,
    dk,
    dv,
    scores,
    probs,
    terms,
    near_sum,
    far_sum,
    whole,
    all_in,
    own_sem,
    seq_send,
    seq_recv,
    in_send,
    in_recv,
    out_send,
    out_recv,
    tap_send,
    tap_recv,
):
    f32, bf16 = jnp.float32, jnp.bfloat16
    data, me = lax.axis_index("dp"), lax.axis_index("seq")
    group = math.isqrt(data_size)
    far, near = data // group, lax.rem(data, group)
    qkv_ref = qkv_ref.at[0]
    rows_here = qkv_ref.shape[0]
    time_rows = rows_here * size
    taps = cw_ref.shape[0]
    margin = (taps - 1) // 2
    part = qkv_ref.shape[1] // 3 // size
    width = part * size
    tiles = part // LANES
    slots = cot.shape[1]
    scale = head_size ** (-0.5)
    to = [lax.rem(me + k, size) for k in range(size)]
    far_order = [0]
    for k in range(1, group // 2 + 1):
        far_order = ([k, group - k] if 2 * k < group else [k]) + far_order

    def partners(e, body):
        for m in range(size):
            for z in far_order:
                if z or m:
                    body(lax.rem(far + z, group) * group + lax.rem(near + e, group), m)

    def neighbours(body):
        for k in range(1, group):
            body(far * group + lax.rem(near + k, group), 0)

    def loop(first, last, body):
        def step(e, carry):
            body(e)
            return carry

        lax.fori_loop(first, last, step, 0)

    def remote(src, dst, send, recv, dp, seq):
        return pltpu.make_async_remote_copy(
            src_ref=src,
            dst_ref=dst,
            send_sem=send,
            recv_sem=recv,
            device_id={"dp": dp, "seq": seq},
            device_id_type=MESH,
        )

    barrier_sem = pltpu.get_barrier_semaphore()

    def greet(dp, m):
        pl.semaphore_signal(
            barrier_sem, inc=1, device_id={"dp": dp, "seq": to[m]}, device_id_type=MESH
        )

    across = [(z, m) for z in range(group) for m in range(size) if z or m]
    neighbours(greet)
    for z, m in across:
        greet(lax.rem(far + z, group) * group + near, m)

    def part_cols(p, d):
        return pl.ds(pl.multiple_of(p * width + d * part, part), part)

    slot = me * data_size + data
    grad_copy = pltpu.make_async_copy(grad_in_ref, grad_ref, own_sem.at[5])
    grad_copy.start()
    counts_copy = pltpu.make_async_copy(counts_in_ref, counts_ref, own_sem.at[7])
    counts_copy.start()
    moves = [(seg_ref.at[0], seg_all.at[me])]
    for p in range(3):
        moves.append(
            (qkv_ref.at[:, part_cols(p, me)], mine.at[rows(me, rows_here), pl.ds(p * part, part)])
        )
    moves.append((weights_ref, cw_ref))
    own = [pltpu.make_async_copy(src, dst, own_sem.at[n]) for n, (src, dst) in enumerate(moves)]
    for copy in own:
        copy.start()
    grad_copy.wait()
    counts_copy.wait()
    slot_row = lax.broadcasted_iota(jnp.int32, sent.shape[1:], 0)

    def mark_empty(j):
        val = jnp.where(slot_row < counts_ref[0, j], grad_ref[0, j].astype(f32), EMPTY)
        sent[j] = val.astype(bf16)

    chunks(data_size, mark_empty)
    own_cot = pltpu.make_async_copy(sent.at[data, :, part_cols(0, me)], cot.at[slot], own_sem.at[6])
    own_cot.start()
    clear(shifted.at[0])
    clear(att_pad)
    clear(dk)
    clear(dv)
    pl.semaphore_wait(barrier_sem, group - 1 + len(across))
    for z, m in across:
        pl.semaphore_signal(
            all_in,
            inc=1,
            device_id={"dp": lax.rem(far + z, group) * group + near, "seq": to[m]},
            device_id_type=MESH,
        )

    halves = ((0, 2 * LANES), (2 * LANES, part - 2 * LANES))

    def seg_copy(k):
        return remote(
            seg_ref.at[0], seg_all.at[me], seq_send.at[k - 1, 6], seq_recv.at[k - 1, 6], data, to[k]
        )

    def seq_copy(k, p, half, first, count):
        start, lanes = halves[half]
        src_col = pl.multiple_of(p * width + to[k] * part + start, LANES)
        return remote(
            qkv_ref.at[pl.ds(first, count), pl.ds(src_col, lanes)],
            mine.at[
                pl.ds(pl.multiple_of(me * rows_here + first, SLICE), count),
                pl.ds(p * part + start, lanes),
            ],
            seq_send.at[k - 1, 3 * half + p],
            seq_recv.at[k - 1, 3 * half + p],
            data,
            to[k],
        )

    def in_copy(half):
        start, lanes = halves[half]

        def copy(dp, m):
            src_col = pl.multiple_of(to[m] * part + start, LANES)
            remote(
                sent.at[dp, :, pl.ds(src_col, lanes)],
                cot.at[slot, :, pl.ds(start, lanes)],
                in_send.at[m, half],
                in_recv.at[m, half],
                dp,
                to[m],
            ).start()

        return copy

    for k in range(1, size):
        seg_copy(k).start()

    pl.semaphore_wait(all_in, len(across))

    def begin(half, slice_rows):
        def step(e):
            for k in range(1, size):
                for p in range(3):
                    first = pl.multiple_of(e * slice_rows, slice_rows)
                    seq_copy(k, p, half, first, slice_rows).start()
            partners(e, in_copy(half))

        loop(0, group, step)
        neighbours(in_copy(half))

    begin(0, SLICE)
    early = group * SLICE
    for p in range(3):
        for k in range(1, size):
            seq_copy(k, p, 0, early, rows_here - early).start()

    def bytes_of(m, ref):
        got = ref.at[pl.ds(0, data_size if m else data_size - 1)]
        return got, got

    for copy in own + [own_cot]:
        copy.wait()
    for k in range(1, size):
        seg_copy(k).wait()
    def in_bytes(m, half):
        return bytes_of(m, out_ref.at[:, 0, pl.ds(0, halves[half][1] // LANES)])

    def cols_of(j):
        return pl.ds(pl.multiple_of(me * part + j * LANES, LANES), LANES)

    def cot_rows(c, j):
        val = cot[rows(c, CH // slots), :, pl.ds(j * LANES, LANES)].astype(f32)
        return val.reshape(CH, LANES)

    def results(first, last):
        def step(c):
            here, there = rows(c, CH), rows(c, CH // slots)
            for j in range(first, last):
                cols = pl.ds(j * LANES, LANES)
                for p, val in enumerate(
                    ((dq_t[cols, here] * scale).T, dk[here, cols] * scale, dv[here, cols])
                ):
                    stage[there, p, j] = val.reshape(CH // slots, slots, LANES).astype(bf16)

        chunks(time_rows // CH, step)

    def out_pair(index, half):
        if half == 0:
            return stage.at[index, :, 0], out_ref.at[data, :, me * tiles]
        here = pl.ds(1, tiles - 1)
        return stage.at[index, :, here], out_ref.at[data, :, pl.ds(me * tiles + 1, tiles - 1)]

    def leave(half):
        def copy(dp, m):
            src, dst = out_pair(to[m] * data_size + dp, half)
            remote(src, dst, out_send.at[m, half], out_recv.at[m, half], dp, to[m]).start()

        return copy, lambda e: partners(e, copy)

    def own_out(half):
        copy = pltpu.make_async_copy(*out_pair(slot, half), own_sem.at[half])
        copy.start()
        return copy

    for half in range(2):
        new = ((0, 1), (2,))[half]
        for m in range(size):
            pltpu.make_async_copy(*in_bytes(m, half), in_recv.at[m, half]).wait()
        if half == 0:
            label_rows(time_rows, cot_rows, seg_all, seg_row, labb)
        convolve(time_rows, new, taps, cols_of, cot_rows, cw_ref, labb, shifted, grad_pad, do_t)
        for k in range(1, size):
            for p in range(3):
                seq_copy(k, p, half, 0, rows_here).wait_recv()
        if half == 0:
            begin(1, rows_here // group)
        flip(time_rows, part, new, mine, k_t, v_t)
        attend(
            half * PAIR,
            time_rows,
            part,
            head_size,
            mine,
            seg_row,
            labb,
            k_t,
            v_t,
            do_t,
            att_t,
            dq_t,
            dk,
            dv,
            scores,
            probs,
        )
        if half == 0:
            results(0, 1)
            own = [own_out(0)]
            neighbours(leave(0)[0])
            loop(0, group, leave(0)[1])
        else:
            results(1, tiles)
            own.append(own_out(1))
            neighbours(leave(1)[0])
            loop(0, group // 2, leave(1)[1])

    spread_rows(
        lambda c, j: att_t[pl.ds(j * LANES, LANES), rows(c, CH)].T, labb, att_pad, time_rows, 0, range(tiles)
    )
    inner = time_rows + GAP * (SEGMENTS - 1)
    each = terms.shape[1]
    terms[group - 1] = jnp.zeros(terms.shape[1:], f32)
    for j in range(tiles):
        cols = pl.ds(j * LANES, LANES)

        def tap_step(c, sums):
            att = att_pad[rows(c, 8), cols]
            return tuple(
                sums[w] + att * tap_view(shifted, margin, w, c * 8, 8, cols) for w in range(taps)
            )

        sums = lax.fori_loop(
            0, inner // 8, tap_step, tuple(jnp.zeros((8, LANES), f32) for _ in range(taps))
        )
        for w in range(taps):
            terms[w // each, w % each : w % each + 1, cols] = jnp.sum(sums[w], axis=0, keepdims=True)

    near_to = [lax.rem(near + k, group) for k in range(group)]
    far_to = [lax.rem(far + k, group) for k in range(group)]
    used = [0]

    def tap_copy(src, dst, z, n, m):
        i = used[0]
        used[0] += 1
        copy = remote(src, dst, tap_send.at[i], tap_recv.at[i], z * group + n, to[m])
        copy.start()
        return copy

    copies = [
        tap_copy(terms.at[near_to[k]], near_sum.at[k - 1], far, near_to[k], 0) for k in range(1, group)
    ]
    loop(group // 2, group - 2, leave(1)[1])
    for copy in copies:
        copy.wait()
    total = terms[near]
    for k in range(1, group):
        total = total + near_sum[k - 1]
    far_sum[far] = total
    copies = [tap_copy(far_sum.at[far], far_sum.at[far], far_to[k], near, 0) for k in range(1, group)]
    loop(group - 2, group, leave(1)[1])
    for copy in copies:
        copy.wait()
    total = far_sum[0]
    for k in range(1, group):
        total = total + far_sum[k]
    whole[me, near] = total * factor
    copies = [
        tap_copy(whole.at[me, near], whole.at[me, near], far, near_to[k], m)
        for k in range(group)
        for m in range(size)
        if k or m
    ]
    for copy in copies:
        copy.wait()
    for m in range(size):
        for g in range(group):
            count = min(each, taps - g * each)
            taps_ref[g * each : g * each + count, m * part : (m + 1) * part] = whole[m, g, :count]

    for copy in own:
        copy.wait()
    for k in range(1, size):
        for p in range(3):
            for half in range(2):
                seq_copy(k, p, half, 0, rows_here).wait_send()
    for m in range(size):
        for half in range(2):
            pltpu.make_async_copy(*in_bytes(m, half), in_send.at[m, half]).wait()
        for half, ref in enumerate((out_ref.at[:, :, 0], out_ref.at[:, :, pl.ds(0, tiles - 1)])):
            pltpu.make_async_copy(*bytes_of(m, ref), out_send.at[m, half]).wait()
            pltpu.make_async_copy(*bytes_of(m, ref), out_recv.at[m, half]).wait()


VMEM = pl.BlockSpec(memory_space=pltpu.VMEM)
ANY = pl.BlockSpec(memory_space=pl.ANY)


def run_block(qkv, grad_in, counts, seg, cw, data_size, size, head_size, factor):
    f32, bf16 = jnp.float32, jnp.bfloat16
    _, rows_here, columns = qkv.shape
    taps = cw.shape[0]
    slots = grad_in.shape[2]
    time_rows, width = rows_here * size, columns // 3 // size
    tiles = width // LANES
    inner = -(-(time_rows + GAP * (SEGMENTS - 1)) // CONV) * CONV
    rows_all = -(-(inner + 2 * GAP) // 48) * 48 + 8
    group = math.isqrt(data_size)
    piece = (group, (taps + 1) // group, width)
    sends = 2 * (group - 1) + group * size - 1
    dma = pltpu.SemaphoreType.DMA
    return pl.pallas_call(
        functools.partial(block_kernel, data_size, size, head_size, factor),
        out_shape=(
            jax.ShapeDtypeStruct((data_size, 3, size * tiles, slots, LANES), bf16),
            jax.ShapeDtypeStruct((taps, width * size), f32),
        ),
        in_specs=[pl.BlockSpec(memory_space=pltpu.HBM)] * 5,
        out_specs=(ANY, VMEM),
        scratch_shapes=[
            pltpu.VMEM((size, 1, rows_here), seg.dtype),
            pltpu.VMEM((time_rows, 3 * width), bf16),
            pltpu.VMEM((1, data_size, slots, size * width), bf16),
            pltpu.SMEM(counts.shape, counts.dtype),
            pltpu.VMEM(cw.shape, f32),
            pltpu.VMEM((data_size, slots, size * width), bf16),
            pltpu.VMEM((data_size * size, slots, width), bf16),
            pltpu.VMEM((data_size * size, 3, tiles, slots, LANES), bf16),
            pltpu.VMEM((1, time_rows), f32),
            pltpu.VMEM((time_rows, LANES), f32),
            pltpu.VMEM((8, rows_all, width), f32),
            pltpu.VMEM((inner, width), f32),
            pltpu.VMEM((rows_all, width), f32),
            pltpu.VMEM((width, time_rows), bf16),
            pltpu.VMEM((width, time_rows), bf16),
            pltpu.VMEM((width, time_rows), bf16),
            pltpu.VMEM((width, time_rows), f32),
            pltpu.VMEM((width, time_rows), f32),
            pltpu.VMEM((time_rows, width), f32),
            pltpu.VMEM((time_rows, width), f32),
            pltpu.VMEM((time_rows, PAIR * TB), f32),
            pltpu.VMEM((time_rows, PAIR * TB), bf16),
            pltpu.VMEM(piece, f32),
            pltpu.VMEM(piece, f32),
            pltpu.VMEM(piece, f32),
            pltpu.VMEM((size,) + piece, f32),
            pltpu.SemaphoreType.REGULAR,
            dma((8,)),
            dma((size - 1, 7)),
            dma((size - 1, 7)),
            dma((size, 2)),
            dma((size, 2)),
            dma((size, 2)),
            dma((size, 2)),
            dma((sends,)),
            dma((sends,)),
        ],
        compiler_params=pltpu.CompilerParams(
            collective_id=1, has_side_effects=True, vmem_limit_bytes=50 * 1024 * 1024
        ),
        cost_estimate=pl.CostEstimate(
            flops=14 * time_rows * time_rows * width, bytes_accessed=64 << 20, transcendentals=0
        ),
    )(qkv, grad_in, counts, seg[None], cw)


def local(qkv, grad_in, counts, segment, conv_weight):
    data_size = lax.axis_size("dp")
    time_size = lax.axis_size("seq")
    width = qkv.shape[2] // 3
    head_size = width // H
    slot_rows = grad_in.shape[2]

    factor = 1.0 / math.sqrt(data_size * slot_rows)
    grads, conv_weight_grad = run_block(
        qkv, grad_in, counts, segment, conv_weight, data_size, time_size, head_size, factor
    )
    qkv_grad = grads.transpose(0, 3, 1, 2, 4).reshape(1, data_size, slot_rows, 3 * width)
    return (qkv_grad, conv_weight_grad)


def solution(mesh):
    in_specs = (
        P("dp", "seq", None),
        P("dp", "seq", None, None),
        P("dp", "seq"),
        P("dp", "seq"),
        P(),
    )
    out_specs = (P("dp", "seq", None, None), P())
    return jax.shard_map(local, mesh=mesh, in_specs=in_specs, out_specs=out_specs, check_vma=False)
```

```python
import functools
import math

import jax
import jax.numpy as jnp
from jax import lax
from jax.experimental import pallas as pl
from jax.experimental.pallas import tpu as pltpu
from jax.sharding import PartitionSpec as P

H = 16

EMPTY = 128.0
EMPTY_ABOVE = 64.0
MASKED = -1e30
LANES = 128
TB = 512
UB = 256
SLICE = 16
CONV = 64
PAIR = 2
GAP = 16
SEGMENTS = 4
MESH = pl.DeviceIdType.MESH
CH = 128


def dot(a, b, contract):
    return lax.dot_general(a, b, (contract, ((), ())), preferred_element_type=jnp.float32)


def rows(index, size):
    return pl.ds(pl.multiple_of(index * size, size), size)


def chunks(count, body):
    def step(index, carry):
        body(index)
        return carry

    lax.fori_loop(0, count, step, 0)


def tap_view(shifted, margin, w, r0, size, cols):
    offset = margin - w
    a, b = offset // 8, offset % 8
    return shifted[b, pl.ds(pl.multiple_of(r0 + GAP + 8 * a, 8), size), cols]


def clear(ref):
    def step(c):
        ref[rows(c, 8), :] = jnp.zeros((8, ref.shape[1]), ref.dtype)

    chunks(ref.shape[0] // 8, step)


def spread_rows(value, labb, target, time_rows, shift, tiles):
    def step(c):
        lab = labb[rows(c, CH), :]
        for j in tiles:
            val = value(c, j)
            for s in range(SEGMENTS):
                there = pl.ds(pl.multiple_of(c * CH + GAP * (s + shift), GAP), CH)
                target[there, pl.ds(j * LANES, LANES)] += jnp.where(lab == s + 1.0, val, 0.0)

    chunks(time_rows // CH, step)


def label_rows(time_rows, cot_rows, seg_ref, seg_row, labb):
    piece = seg_ref.shape[2]
    for s in range(seg_ref.shape[0]):
        seg_row[:, s * piece : (s + 1) * piece] = seg_ref[s].astype(jnp.float32)

    def label(c):
        here = rows(c, CH)
        across = jnp.broadcast_to(seg_row[:, here], (CH, CH)).T
        labb[here, :] = jnp.where(cot_rows(c, 0) < EMPTY_ABOVE, across + 1.0, 0.0)

    chunks(time_rows // CH, label)


def convolve(time_rows, tiles, taps, cols_of, cot_rows, cw_ref, labb, shifted, grad_pad, do_t):
    f32 = jnp.float32
    margin = (taps - 1) // 2
    spread_rows(cot_rows, labb, shifted.at[0], time_rows, 1, tiles)

    def shift(c):
        r0 = pl.multiple_of(c * 48, 8)
        for j in tiles:
            cols = pl.ds(j * LANES, LANES)
            block = shifted[0, pl.ds(r0, 56), cols]
            for b in range(1, 8):
                shifted[b, pl.ds(r0, 48), cols] = block[b : b + 48]

    chunks((shifted.shape[1] - 8) // 48, shift)

    def conv(c):
        r0 = pl.multiple_of(c * CONV, CONV)
        for j in tiles:
            cols = pl.ds(j * LANES, LANES)
            total = jnp.zeros((CONV, LANES), f32)
            for b in range(8):
                block = shifted[b, pl.ds(r0, CONV + 2 * GAP - 8), cols]
                for a in range(-2, 2):
                    w = margin - 8 * a - b
                    if 0 <= w < taps:
                        weight = cw_ref[w : w + 1, cols_of(j)]
                        total = total + weight * block[GAP + 8 * a : GAP + 8 * a + CONV]
            grad_pad[pl.ds(r0, CONV), cols] = total

    chunks(grad_pad.shape[0] // CONV, conv)

    def collect(c):
        lab = labb[rows(c, CH), :]
        for j in tiles:
            cols = pl.ds(j * LANES, LANES)
            total = jnp.zeros((CH, LANES), f32)
            for s in range(SEGMENTS):
                there = pl.ds(pl.multiple_of(c * CH + GAP * s, GAP), CH)
                total = total + jnp.where(lab == s + 1.0, grad_pad[there, cols], 0.0)
            do_t[cols, rows(c, CH)] = total.astype(jnp.bfloat16).T

    chunks(time_rows // CH, collect)


def flip(time_rows, width, tiles, qkv_ref, k_t, v_t):
    def step(c):
        here = rows(c, CH)
        for j in tiles:
            for n, target in ((1, k_t), (2, v_t)):
                block = qkv_ref[here, pl.ds(n * width + j * LANES, LANES)]
                target[pl.ds(j * LANES, LANES), here] = block.T

    chunks(time_rows // CH, step)


def attend(
    h0, time_rows, width, head_size, qkv_ref, seg_row, labb, k_t, v_t, do_t, att_t, dq_t, dk, dv, scores, probs
):
    f32, bf16 = jnp.float32, jnp.bfloat16
    scale = head_size ** (-0.5)
    cols_here = PAIR * TB
    row_index = lax.broadcasted_iota(jnp.int32, (UB, cols_here), 0)
    col_index = lax.broadcasted_iota(jnp.int32, (UB, cols_here), 1) % TB
    apart = col_index - row_index
    to_exp2 = scale * math.log2(math.e)

    first, last = h0 * head_size, (h0 + PAIR) * head_size
    lane0 = first // LANES * LANES
    span = -(-last // LANES) * LANES - lane0
    lane = lax.broadcasted_iota(jnp.int32, (TB, span), 1) + lane0
    head_rows = [pl.ds((h0 + n) * head_size, head_size) for n in range(PAIR)]

    def beside(values):
        return jnp.concatenate(values, axis=1)

    def time_block(tb, carry):
        here = rows(tb, TB)
        q = qkv_ref[here, pl.ds(lane0, span)]
        q = jnp.concatenate(
            [
                jnp.where(
                    (lane >= (h0 + n) * head_size) & (lane < (h0 + n + 1) * head_size),
                    q,
                    jnp.zeros((), bf16),
                )
                for n in range(PAIR)
            ],
            axis=0,
        )
        want = beside([seg_row[:, here] + 1.0] * PAIR)

        def score_step(ub, highest):
            keys = rows(ub, UB)
            s = dot(qkv_ref[keys, pl.ds(width + lane0, span)], q, ((1,), (1,)))
            lab = beside([labb[keys, :]] * (cols_here // LANES))
            ok = (lab == want) | (apart == ub * UB - tb * TB)
            s = jnp.where(ok, s, MASKED)
            scores[keys, :] = s
            return jnp.maximum(highest, jnp.max(s.reshape(UB // 8, 8, cols_here), axis=0))

        highest = lax.fori_loop(0, time_rows // UB, score_step, jnp.full((8, cols_here), MASKED, f32), unroll=True)
        highest = jnp.max(highest, axis=0, keepdims=True) * to_exp2
        for n in range(PAIR):
            att_t[head_rows[n], here] = jnp.zeros((head_size, TB), f32)
            dq_t[head_rows[n], here] = jnp.zeros((head_size, TB), f32)

        def soft_step(ub, total):
            keys = rows(ub, UB)
            p = jnp.exp2(scores[keys, :] * to_exp2 - highest)
            total = total + jnp.sum(p.reshape(UB // 8, 8, cols_here), axis=0)
            p = p.astype(bf16)
            probs[keys, :] = p
            for n in range(PAIR):
                att_t[head_rows[n], here] += dot(
                    v_t[head_rows[n], keys], p[:, n * TB : (n + 1) * TB], ((1,), (0,))
                )
            return total

        total = lax.fori_loop(0, time_rows // UB, soft_step, jnp.zeros((8, cols_here), f32), unroll=True)
        inverse = 1.0 / jnp.sum(total, axis=0, keepdims=True)
        deltas, wide = [], []
        for n in range(PAIR):
            inv = inverse[:, n * TB : (n + 1) * TB]
            att = (att_t[head_rows[n], here] * inv).astype(bf16).astype(f32)
            att_t[head_rows[n], here] = att
            do = do_t[head_rows[n], here].astype(f32)
            deltas.append(jnp.sum(do * att, axis=0, keepdims=True) * inv)
            before = (h0 + n) * head_size - lane0
            after = span - before - head_size
            parts = [(do * inv).astype(bf16)]
            if before:
                parts = [jnp.zeros((before, TB), bf16)] + parts
            if after:
                parts = parts + [jnp.zeros((after, TB), bf16)]
            wide.append(jnp.concatenate(parts, axis=0))
        delta, do_wide = beside(deltas), beside(wide)

        def grad_step(ub, carry):
            keys = rows(ub, UB)
            p = probs[keys, :]
            dp = dot(qkv_ref[keys, pl.ds(2 * width + lane0, span)], do_wide, ((1,), (0,)))
            ds = (p.astype(f32) * (dp - delta)).astype(bf16)
            dk[keys, pl.ds(lane0, span)] += dot(ds, q, ((1,), (0,)))
            dv[keys, pl.ds(lane0, span)] += dot(p, do_wide, ((1,), (1,)))
            for n in range(PAIR):
                dq_t[head_rows[n], here] += dot(
                    k_t[head_rows[n], keys], ds[:, n * TB : (n + 1) * TB], ((1,), (0,))
                )
            return carry

        lax.fori_loop(0, time_rows // UB, grad_step, 0, unroll=True)
        return carry

    lax.fori_loop(0, time_rows // TB, time_block, 0, unroll=True)


def block_kernel(
    data_size,
    size,
    head_size,
    factor,
    qkv_ref,
    grad_in_ref,
    counts_in_ref,
    seg_ref,
    weights_ref,
    out_ref,
    taps_ref,
    seg_all,
    mine,
    grad_ref,
    counts_ref,
    cw_ref,
    sent,
    cot,
    stage,
    seg_row,
    labb,
    shifted,
    grad_pad,
    att_pad,
    k_t,
    v_t,
    do_t,
    att_t,
    dq_t,
    dk,
    dv,
    scores,
    probs,
    terms,
    near_sum,
    far_sum,
    whole,
    all_in,
    own_sem,
    seq_send,
    seq_recv,
    in_send,
    in_recv,
    out_send,
    out_recv,
    tap_send,
    tap_recv,
):
    f32, bf16 = jnp.float32, jnp.bfloat16
    data, me = lax.axis_index("dp"), lax.axis_index("seq")
    group = math.isqrt(data_size)
    far, near = data // group, lax.rem(data, group)
    qkv_ref = qkv_ref.at[0]
    rows_here = qkv_ref.shape[0]
    time_rows = rows_here * size
    taps = cw_ref.shape[0]
    margin = (taps - 1) // 2
    part = qkv_ref.shape[1] // 3 // size
    width = part * size
    tiles = part // LANES
    slots = cot.shape[1]
    scale = head_size ** (-0.5)
    to = [lax.rem(me + k, size) for k in range(size)]
    far_order = [0]
    for k in range(1, group // 2 + 1):
        far_order = ([k, group - k] if 2 * k < group else [k]) + far_order

    def partners(e, body):
        for m in range(size):
            for z in far_order:
                if z or m:
                    body(lax.rem(far + z, group) * group + lax.rem(near + e, group), m)

    def neighbours(body):
        for k in range(1, group):
            body(far * group + lax.rem(near + k, group), 0)

    def loop(first, last, body):
        def step(e, carry):
            body(e)
            return carry

        lax.fori_loop(first, last, step, 0)

    def remote(src, dst, send, recv, dp, seq):
        return pltpu.make_async_remote_copy(
            src_ref=src,
            dst_ref=dst,
            send_sem=send,
            recv_sem=recv,
            device_id={"dp": dp, "seq": seq},
            device_id_type=MESH,
        )

    barrier_sem = pltpu.get_barrier_semaphore()

    def greet(dp, m):
        pl.semaphore_signal(
            barrier_sem, inc=1, device_id={"dp": dp, "seq": to[m]}, device_id_type=MESH
        )

    across = [(z, m) for z in range(group) for m in range(size) if z or m]
    neighbours(greet)
    for z, m in across:
        greet(lax.rem(far + z, group) * group + near, m)

    def part_cols(p, d):
        return pl.ds(pl.multiple_of(p * width + d * part, part), part)

    slot = me * data_size + data
    grad_copy = pltpu.make_async_copy(grad_in_ref, grad_ref, own_sem.at[5])
    grad_copy.start()
    counts_copy = pltpu.make_async_copy(counts_in_ref, counts_ref, own_sem.at[7])
    counts_copy.start()
    moves = [(seg_ref.at[0], seg_all.at[me])]
    for p in range(3):
        moves.append(
            (qkv_ref.at[:, part_cols(p, me)], mine.at[rows(me, rows_here), pl.ds(p * part, part)])
        )
    moves.append((weights_ref, cw_ref))
    own = [pltpu.make_async_copy(src, dst, own_sem.at[n]) for n, (src, dst) in enumerate(moves)]
    for copy in own:
        copy.start()
    pl.semaphore_wait(barrier_sem, group - 1 + len(across))
    for z, m in across:
        pl.semaphore_signal(
            all_in,
            inc=1,
            device_id={"dp": lax.rem(far + z, group) * group + near, "seq": to[m]},
            device_id_type=MESH,
        )
    grad_copy.wait()
    counts_copy.wait()
    slot_row = lax.broadcasted_iota(jnp.int32, sent.shape[1:], 0)

    def mark_empty(j):
        val = jnp.where(slot_row < counts_ref[0, j], grad_ref[0, j].astype(f32), EMPTY)
        sent[j] = val.astype(bf16)

    chunks(data_size, mark_empty)
    own_cot = pltpu.make_async_copy(sent.at[data, :, part_cols(0, me)], cot.at[slot], own_sem.at[6])
    own_cot.start()
    halves = ((0, 2 * LANES), (2 * LANES, part - 2 * LANES))

    def seg_copy(k):
        return remote(
            seg_ref.at[0], seg_all.at[me], seq_send.at[k - 1, 6], seq_recv.at[k - 1, 6], data, to[k]
        )

    def seq_copy(k, p, half, first, count):
        start, lanes = halves[half]
        src_col = pl.multiple_of(p * width + to[k] * part + start, LANES)
        return remote(
            qkv_ref.at[pl.ds(first, count), pl.ds(src_col, lanes)],
            mine.at[
                pl.ds(pl.multiple_of(me * rows_here + first, SLICE), count),
                pl.ds(p * part + start, lanes),
            ],
            seq_send.at[k - 1, 3 * half + p],
            seq_recv.at[k - 1, 3 * half + p],
            data,
            to[k],
        )

    def in_copy(half):
        start, lanes = halves[half]

        def copy(dp, m):
            src_col = pl.multiple_of(to[m] * part + start, LANES)
            remote(
                sent.at[dp, :, pl.ds(src_col, lanes)],
                cot.at[slot, :, pl.ds(start, lanes)],
                in_send.at[m, half],
                in_recv.at[m, half],
                dp,
                to[m],
            ).start()

        return copy

    for k in range(1, size):
        seg_copy(k).start()

    pl.semaphore_wait(all_in, len(across))

    def begin(half, slice_rows):
        def step(e):
            for k in range(1, size):
                for p in range(3):
                    first = pl.multiple_of(e * slice_rows, slice_rows)
                    seq_copy(k, p, half, first, slice_rows).start()
            partners(e, in_copy(half))

        loop(0, group, step)
        neighbours(in_copy(half))

    begin(0, SLICE)
    early = group * SLICE
    for p in range(3):
        for k in range(1, size):
            seq_copy(k, p, 0, early, rows_here - early).start()
    clear(shifted.at[0])
    clear(att_pad)
    clear(dk)
    clear(dv)

    def bytes_of(m, ref):
        got = ref.at[pl.ds(0, data_size if m else data_size - 1)]
        return got, got

    for copy in own + [own_cot]:
        copy.wait()
    for k in range(1, size):
        seg_copy(k).wait()
    def in_bytes(m, half):
        return bytes_of(m, out_ref.at[:, 0, pl.ds(0, halves[half][1] // LANES)])

    def cols_of(j):
        return pl.ds(pl.multiple_of(me * part + j * LANES, LANES), LANES)

    def cot_rows(c, j):
        val = cot[rows(c, CH // slots), :, pl.ds(j * LANES, LANES)].astype(f32)
        return val.reshape(CH, LANES)

    def results(first, last):
        def step(c):
            here, there = rows(c, CH), rows(c, CH // slots)
            for j in range(first, last):
                cols = pl.ds(j * LANES, LANES)
                for p, val in enumerate(
                    ((dq_t[cols, here] * scale).T, dk[here, cols] * scale, dv[here, cols])
                ):
                    stage[there, p, j] = val.reshape(CH // slots, slots, LANES).astype(bf16)

        chunks(time_rows // CH, step)

    def out_pair(index, half):
        if half == 0:
            return stage.at[index, :, 0], out_ref.at[data, :, me * tiles]
        here = pl.ds(1, tiles - 1)
        return stage.at[index, :, here], out_ref.at[data, :, pl.ds(me * tiles + 1, tiles - 1)]

    def leave(half):
        def copy(dp, m):
            src, dst = out_pair(to[m] * data_size + dp, half)
            remote(src, dst, out_send.at[m, half], out_recv.at[m, half], dp, to[m]).start()

        return copy, lambda e: partners(e, copy)

    def own_out(half):
        copy = pltpu.make_async_copy(*out_pair(slot, half), own_sem.at[half])
        copy.start()
        return copy

    for half in range(2):
        new = ((0, 1), (2,))[half]
        for m in range(size):
            pltpu.make_async_copy(*in_bytes(m, half), in_recv.at[m, half]).wait()
        if half == 0:
            label_rows(time_rows, cot_rows, seg_all, seg_row, labb)
        convolve(time_rows, new, taps, cols_of, cot_rows, cw_ref, labb, shifted, grad_pad, do_t)
        for k in range(1, size):
            for p in range(3):
                seq_copy(k, p, half, 0, rows_here).wait_recv()
        if half == 0:
            begin(1, rows_here // group)
        flip(time_rows, part, new, mine, k_t, v_t)
        attend(
            half * PAIR,
            time_rows,
            part,
            head_size,
            mine,
            seg_row,
            labb,
            k_t,
            v_t,
            do_t,
            att_t,
            dq_t,
            dk,
            dv,
            scores,
            probs,
        )
        if half == 0:
            results(0, 1)
            own = [own_out(0)]
            neighbours(leave(0)[0])
            loop(0, group, leave(0)[1])
        else:
            results(1, tiles)
            own.append(own_out(1))
            neighbours(leave(1)[0])
            loop(0, group // 2, leave(1)[1])

    spread_rows(
        lambda c, j: att_t[pl.ds(j * LANES, LANES), rows(c, CH)].T, labb, att_pad, time_rows, 0, range(tiles)
    )
    inner = time_rows + GAP * (SEGMENTS - 1)
    each = terms.shape[1]
    terms[group - 1] = jnp.zeros(terms.shape[1:], f32)
    for j in range(tiles):
        cols = pl.ds(j * LANES, LANES)

        def tap_step(c, sums):
            att = att_pad[rows(c, 8), cols]
            return tuple(
                sums[w] + att * tap_view(shifted, margin, w, c * 8, 8, cols) for w in range(taps)
            )

        sums = lax.fori_loop(
            0, inner // 8, tap_step, tuple(jnp.zeros((8, LANES), f32) for _ in range(taps))
        )
        for w in range(taps):
            terms[w // each, w % each : w % each + 1, cols] = jnp.sum(sums[w], axis=0, keepdims=True)

    near_to = [lax.rem(near + k, group) for k in range(group)]
    far_to = [lax.rem(far + k, group) for k in range(group)]
    used = [0]

    def tap_copy(src, dst, z, n, m):
        i = used[0]
        used[0] += 1
        copy = remote(src, dst, tap_send.at[i], tap_recv.at[i], z * group + n, to[m])
        copy.start()
        return copy

    copies = [
        tap_copy(terms.at[near_to[k]], near_sum.at[k - 1], far, near_to[k], 0) for k in range(1, group)
    ]
    loop(group // 2, group - 2, leave(1)[1])
    for copy in copies:
        copy.wait()
    total = terms[near]
    for k in range(1, group):
        total = total + near_sum[k - 1]
    far_sum[far] = total
    copies = [tap_copy(far_sum.at[far], far_sum.at[far], far_to[k], near, 0) for k in range(1, group)]
    loop(group - 2, group, leave(1)[1])
    for copy in copies:
        copy.wait()
    total = far_sum[0]
    for k in range(1, group):
        total = total + far_sum[k]
    whole[me, near] = total * factor
    copies = [
        tap_copy(whole.at[me, near], whole.at[me, near], far, near_to[k], m)
        for k in range(group)
        for m in range(size)
        if k or m
    ]
    for copy in copies:
        copy.wait()
    for m in range(size):
        for g in range(group):
            count = min(each, taps - g * each)
            taps_ref[g * each : g * each + count, m * part : (m + 1) * part] = whole[m, g, :count]

    for copy in own:
        copy.wait()
    for k in range(1, size):
        for p in range(3):
            for half in range(2):
                seq_copy(k, p, half, 0, rows_here).wait_send()
    for m in range(size):
        for half in range(2):
            pltpu.make_async_copy(*in_bytes(m, half), in_send.at[m, half]).wait()
        for half, ref in enumerate((out_ref.at[:, :, 0], out_ref.at[:, :, pl.ds(0, tiles - 1)])):
            pltpu.make_async_copy(*bytes_of(m, ref), out_send.at[m, half]).wait()
            pltpu.make_async_copy(*bytes_of(m, ref), out_recv.at[m, half]).wait()


VMEM = pl.BlockSpec(memory_space=pltpu.VMEM)
ANY = pl.BlockSpec(memory_space=pl.ANY)


def run_block(qkv, grad_in, counts, seg, cw, data_size, size, head_size, factor):
    f32, bf16 = jnp.float32, jnp.bfloat16
    _, rows_here, columns = qkv.shape
    taps = cw.shape[0]
    slots = grad_in.shape[2]
    time_rows, width = rows_here * size, columns // 3 // size
    tiles = width // LANES
    inner = -(-(time_rows + GAP * (SEGMENTS - 1)) // CONV) * CONV
    rows_all = -(-(inner + 2 * GAP) // 48) * 48 + 8
    group = math.isqrt(data_size)
    piece = (group, (taps + 1) // group, width)
    sends = 2 * (group - 1) + group * size - 1
    dma = pltpu.SemaphoreType.DMA
    return pl.pallas_call(
        functools.partial(block_kernel, data_size, size, head_size, factor),
        out_shape=(
            jax.ShapeDtypeStruct((data_size, 3, size * tiles, slots, LANES), bf16),
            jax.ShapeDtypeStruct((taps, width * size), f32),
        ),
        in_specs=[pl.BlockSpec(memory_space=pltpu.HBM)] * 5,
        out_specs=(ANY, VMEM),
        scratch_shapes=[
            pltpu.VMEM((size, 1, rows_here), seg.dtype),
            pltpu.VMEM((time_rows, 3 * width), bf16),
            pltpu.VMEM((1, data_size, slots, size * width), bf16),
            pltpu.SMEM(counts.shape, counts.dtype),
            pltpu.VMEM(cw.shape, f32),
            pltpu.VMEM((data_size, slots, size * width), bf16),
            pltpu.VMEM((data_size * size, slots, width), bf16),
            pltpu.VMEM((data_size * size, 3, tiles, slots, LANES), bf16),
            pltpu.VMEM((1, time_rows), f32),
            pltpu.VMEM((time_rows, LANES), f32),
            pltpu.VMEM((8, rows_all, width), f32),
            pltpu.VMEM((inner, width), f32),
            pltpu.VMEM((rows_all, width), f32),
            pltpu.VMEM((width, time_rows), bf16),
            pltpu.VMEM((width, time_rows), bf16),
            pltpu.VMEM((width, time_rows), bf16),
            pltpu.VMEM((width, time_rows), f32),
            pltpu.VMEM((width, time_rows), f32),
            pltpu.VMEM((time_rows, width), f32),
            pltpu.VMEM((time_rows, width), f32),
            pltpu.VMEM((time_rows, PAIR * TB), f32),
            pltpu.VMEM((time_rows, PAIR * TB), bf16),
            pltpu.VMEM(piece, f32),
            pltpu.VMEM(piece, f32),
            pltpu.VMEM(piece, f32),
            pltpu.VMEM((size,) + piece, f32),
            pltpu.SemaphoreType.REGULAR,
            dma((8,)),
            dma((size - 1, 7)),
            dma((size - 1, 7)),
            dma((size, 2)),
            dma((size, 2)),
            dma((size, 2)),
            dma((size, 2)),
            dma((sends,)),
            dma((sends,)),
        ],
        compiler_params=pltpu.CompilerParams(
            collective_id=1, has_side_effects=True, vmem_limit_bytes=50 * 1024 * 1024
        ),
        cost_estimate=pl.CostEstimate(
            flops=14 * time_rows * time_rows * width, bytes_accessed=64 << 20, transcendentals=0
        ),
    )(qkv, grad_in, counts, seg[None], cw)


def local(qkv, grad_in, counts, segment, conv_weight):
    data_size = lax.axis_size("dp")
    time_size = lax.axis_size("seq")
    width = qkv.shape[2] // 3
    head_size = width // H
    slot_rows = grad_in.shape[2]

    factor = 1.0 / math.sqrt(data_size * slot_rows)
    grads, conv_weight_grad = run_block(
        qkv, grad_in, counts, segment, conv_weight, data_size, time_size, head_size, factor
    )
    qkv_grad = grads.transpose(0, 3, 1, 2, 4).reshape(1, data_size, slot_rows, 3 * width)
    return (qkv_grad, conv_weight_grad)


def solution(mesh):
    in_specs = (
        P("dp", "seq", None),
        P("dp", "seq", None, None),
        P("dp", "seq"),
        P("dp", "seq"),
        P(),
    )
    out_specs = (P("dp", "seq", None, None), P())
    return jax.shard_map(local, mesh=mesh, in_specs=in_specs, out_specs=out_specs, check_vma=False)
```
